32 devices in a mesh: groups: 2 (over y), ep: 4 (over z), tp: 2 (over x), sp: 2 (over core).
Axes of the slice: x: 2, y: 2, z: 4, core: 2. Of those that a mesh axis runs over, the one named last changes fastest.
Arguments:
- query: bfloat16 [512, 4096], P(('groups', 'ep', 'sp'), 'tp'), parts along dimension 0, may hold values from -80 to 80
- key_cache: bfloat16 [512, 256, 512], P(('groups', 'ep', 'sp')), parts along dimension 0, may hold values from -4.5 to 4.5
- value_cache: bfloat16 [512, 256, 512], P(('groups', 'ep', 'sp')), parts along dimension 0, may hold values from -6 to 6
- new_key: bfloat16 [512, 512], P(('groups', 'ep', 'sp')), parts along dimension 0, may hold values from -4.5 to 4.5
- new_value: bfloat16 [512, 512], P(('groups', 'ep', 'sp')), parts along dimension 0, may hold values from -6 to 6
- lengths: int32 [512], P(('groups', 'ep', 'sp')), parts along dimension 0, may hold values from 1 to 256, as said below
- out_weight: bfloat16 [4096, 2048], P('tp', 'sp'), may hold values from -0.09375 to 0.09375
- residual: bfloat16 [512, 2048], P(('groups', 'ep', 'sp')), parts along dimension 0, may hold values from -6 to 6
- norm_gain: float32 [2048], replicated, may hold values from 0.25 to 1.75
- expert_ids: int32 [512, 8], P(('groups', 'ep', 'sp')), parts along dimension 0, may hold values from 0 to 15, all different within a row; in each aligned block of 32 rows (0 to 31, 32 to 63, ...) at most 32 rows name the same one
- gate_weights: float32 [512, 8], P(('groups', 'ep', 'sp')), parts along dimension 0, may hold values from 0.05 to 1
- w_gate: bfloat16 [16, 2048, 1024], P(('ep', 'sp'), None, 'tp'), may hold values from -0.125 to 0.125
- w_up: bfloat16 [16, 2048, 1024], P(('ep', 'sp'), None, 'tp'), may hold values from -0.125 to 0.125
- w_down: bfloat16 [16, 1024, 2048], P(('ep', 'sp'), 'tp'), may hold values from -0.1875 to 0.1875
Outputs:
- layer_out: bfloat16 [512, 2048], P(('groups', 'ep', 'sp'), 'tp'), parts along dimension 0
The draws below stay inside these ranges and needn't reach their ends.
There are 2 independent parts, one for each index of `groups`. The reference program is written for one: setup_inputs(seed, part) draws one part's arguments, and reference() takes and returns one part's arrays. A program takes and returns all parts, laid end to end along the dimension named above; an argument that names none is the same for every part. Nothing has to cross between parts.
Inputs may be any that keep to these rules, and one draw needn't show every extreme that they name: `expert_ids`: each row names 8 different experts; within each aligned block of 32 rows (the rows of one device), no expert is named by more than 32 rows, and in every draw some expert is named by exactly 32 rows of some block. `lengths`: one request in every draw has all 256 positions valid.
All inputs are finite; a program needn't handle non-finite values.
Results may differ from the reference program's by a relative error of at most 0.0056.
Values may be sent and summed in bfloat16 or wider, within the bound.
No kernel may reach another device: no remote copies, remote signals or barrier semaphores. Data moves between devices by JAX's collectives and lax.ppermute only.
A program may use at most 128 MiB of HBM per device.

```python
import math
import jax
import jax.numpy as jnp
import numpy as np
from jax import lax

D = 2048
HEADS = 32
KV_HEADS = 4
HD = 128
FF = 1024
TOP = 8
LEN = 256
REQUESTS = 256
ROWS_DEV = 32
EXPERTS = 16
CAP = 32
N_TP = 2


def draw_query(key, part):
    key = jax.random.fold_in(key, 21)
    key_entries = jax.random.fold_in(key, 0)
    drawn_draw = jnp.clip(jax.random.normal(key_entries, (REQUESTS, HEADS * HD), jnp.float32), -6.0, 6.0)
    return drawn_draw.astype(jnp.bfloat16)


def draw_key_cache(key, part):
    key = jax.random.fold_in(key, 22)
    drawn_draw = jnp.clip(jax.random.normal(key, (REQUESTS, LEN, KV_HEADS * HD), jnp.float32), -4.5, 4.5)
    return drawn_draw.astype(jnp.bfloat16)


def draw_new_key(key, part):
    key = jax.random.fold_in(key, 23)
    drawn_draw = jnp.clip(jax.random.normal(key, (REQUESTS, KV_HEADS * HD), jnp.float32), -4.5, 4.5)
    return drawn_draw.astype(jnp.bfloat16)


def draw_lengths(key, part):
    key = jax.random.fold_in(key, 24)
    key_drawn, key_longest = jax.random.split(key, 2)
    drawn_lengths = jax.random.randint(key_drawn, (REQUESTS,), 1, LEN + 1)
    longest = jax.random.randint(key_longest, (), 0, REQUESTS)
    return jnp.where(jnp.arange(REQUESTS) == longest, LEN, drawn_lengths).astype(jnp.int32)


def shard_levels(stream_key, dims, pieces, least, largest):
    level = 1.0
    for axis_at, blocks in pieces:
        heights = jax.random.uniform(jax.random.fold_in(jax.random.fold_in(stream_key, 6), axis_at), (blocks,), jnp.float32, least / len(pieces), largest / len(pieces))
        level = level * jnp.repeat(jnp.exp(heights), dims[axis_at] // blocks).reshape((-1,) + (1,) * (len(dims) - 1 - axis_at))
    return level


def deal_out(rng, own, number, rows, number_of, top, limit, slope):
    order = jax.random.permutation(rng, number_of)
    packed, usual = load_shares(number_of, rows * top, limit, slope, True), load_shares(number_of, rows * top, limit, slope, False)
    places = jnp.arange(number_of)

    def named(sizes, turn):
        used = int((sizes > 0).sum())
        fixed = max(1, used // 4)
        passed = fixed + (places - fixed + turn * (used - fixed)) % max(1, number_of - fixed)
        return jnp.zeros((number_of,), jnp.int32).at[order[jnp.where(places < fixed, places, passed)]].set(jnp.asarray(sizes, jnp.int32))

    sizes = jnp.where(number % 4 == 0, named(packed, number // 4), named(usual, number - number // 4 - 1))
    mixed = jax.random.permutation(jax.random.fold_in(own, 3), number_of)
    donor, sink = mixed[0:number_of // 2 * 2:2], mixed[1:number_of // 2 * 2:2]
    room = jnp.minimum(sizes[donor] - 1, limit - sizes[sink]) // 2
    room = jnp.where((donor == order[0]) | (sink == order[0]) | (sizes[sink] == 0), 0, jnp.maximum(room, 0))
    passed = jax.random.randint(jax.random.fold_in(own, 4), (number_of // 2,), 0, 1 << 20) % (room + 1)
    sizes = sizes.at[donor].add(-passed).at[sink].add(passed)
    labels = jnp.searchsorted(jnp.cumsum(sizes), jnp.arange(rows * top), side="right").astype(jnp.int32)
    table = labels.reshape(top, rows).T
    table = table[jax.random.permutation(jax.random.fold_in(own, 1), rows)]
    turn = jax.random.randint(jax.random.fold_in(own, 2), (rows, 1), 0, top)
    return jnp.take_along_axis(table, (jnp.arange(top)[None, :] + turn) % top, axis=1)


def load_shares(number_of, total, reach, slope, full):
    portions = [(1 << 20) // math.isqrt(grade ** slope) + 1 for grade in range(1, number_of + 1)]
    largest = reach if full else min(reach, max(-(-total // number_of), total * portions[0] // sum(portions)))
    least = 1 if total - largest >= number_of - 1 else 0
    counts, spare = [largest] + [least] * (number_of - 1), total - largest - least * (number_of - 1)
    while spare > 0:
        free = [i for i in range(1, number_of) if counts[i] < largest] or [i for i in range(1, number_of) if counts[i] < reach]
        pool, budget = sum([portions[i] for i in free]), spare
        for i in free:
            extra = min(reach - counts[i], max(1, budget * portions[i] // pool), spare)
            counts[i] = counts[i] + extra
            spare = spare - extra
    return np.array(counts)


def bell_draw(key, dims, width, reach, pieces=(), kind=jnp.bfloat16):
    entries = width * jax.random.normal(key, dims, jnp.float32)
    if pieces:
        entries = entries * shard_levels(key, dims, pieces, -0.22, 0.18)
    return jnp.clip(entries, -reach, reach).astype(kind)


def setup_inputs(seed: int = 0, part: int = 0) -> dict:
    seeds = jax.random.split(jax.random.key(seed), 15)
    part_keys = jax.random.split(jax.random.fold_in(seeds[14], part), 15)
    query = draw_query(jax.random.fold_in(jax.random.fold_in(seeds[14], part), 71), part)
    key_cache = draw_key_cache(jax.random.fold_in(jax.random.fold_in(seeds[14], part), 71), part)
    value_cache = bell_draw(part_keys[2], (REQUESTS, LEN, KV_HEADS * HD), 1.0, 6.0, ((0, 8),))
    new_key = draw_new_key(jax.random.fold_in(jax.random.fold_in(seeds[14], part), 71), part)
    new_value = bell_draw(part_keys[4], (REQUESTS, KV_HEADS * HD), 1.0, 6.0, ((0, 8),))
    lengths = draw_lengths(jax.random.fold_in(jax.random.fold_in(seeds[14], part), 71), part)
    out_weight = bell_draw(seeds[6], (HEADS * HD, D), (HEADS * HD) ** -0.5, 0.09375, ((0, 2), (1, 2)))
    residual = bell_draw(part_keys[7], (REQUESTS, D), 1.0, 6.0, ((0, 8),))
    norm_gain = jnp.clip(1.0 + 0.15 * jax.random.normal(seeds[8], (D,), jnp.float32), 0.25, 1.75)
    expert_ids_keys = jax.random.split(jax.random.fold_in(part_keys[9], 1), REQUESTS // ROWS_DEV)
    expert_ids_turns = jax.random.permutation(jax.random.fold_in(part_keys[9], 3), REQUESTS // ROWS_DEV)
    expert_ids = jax.vmap(lambda own, number: deal_out(jax.random.fold_in(part_keys[9], 2), own, number, ROWS_DEV, EXPERTS, TOP, CAP, 2))(expert_ids_keys, expert_ids_turns).reshape((REQUESTS, TOP))
    gate_weights = jnp.clip(jnp.exp(math.log(1.0) - 2.9957323 * jax.random.uniform(part_keys[10], (REQUESTS, TOP), jnp.float32) ** shard_levels(part_keys[10], (REQUESTS, TOP), ((0, 8),), -0.2, 0.2)), 0.05, 1.0)
    w_gate = bell_draw(seeds[11], (EXPERTS, D, FF), D ** -0.5, 0.125, ((0, 8), (2, 2)))
    w_up = bell_draw(seeds[12], (EXPERTS, D, FF), D ** -0.5, 0.125, ((0, 8), (2, 2)))
    w_down = bell_draw(seeds[13], (EXPERTS, FF, D), FF ** -0.5, 0.1875, ((0, 8), (1, 2)))
    return {"query": query, "key_cache": key_cache, "value_cache": value_cache, "new_key": new_key, "new_value": new_value, "lengths": lengths, "out_weight": out_weight, "residual": residual, "norm_gain": norm_gain, "expert_ids": expert_ids, "gate_weights": gate_weights, "w_gate": w_gate, "w_up": w_up, "w_down": w_down}


masked_fill = -1e+30
norm_epsilon = 1e-06

def merge_pair(first_state, second_state):
    peak = jnp.maximum(first_state[0], second_state[0])
    left_factor = jnp.exp(first_state[0] - peak)
    right_factor = jnp.exp(second_state[0] - peak)
    weight_sum = first_state[1] * left_factor + second_state[1] * right_factor
    blended = first_state[2] * left_factor[..., None] + second_state[2] * right_factor[..., None]
    return (peak, weight_sum, blended)

def block_softmax(queries, key_rows, value_rows, visible, scaling):
    scores = jnp.einsum('rkgd,rtkd->rkgt', queries.astype(jnp.float32), key_rows.astype(jnp.float32)) * scaling
    scores = jnp.where(visible[:, None, None, :], scores, masked_fill)
    peak = lax.optimization_barrier(jnp.max(scores, axis=-1))
    probabilities = jnp.where(visible[:, None, None, :], jnp.exp(scores - peak[..., None]), 0.0)
    weight_sum = lax.optimization_barrier(jnp.sum(probabilities, axis=-1))
    rounded = lax.optimization_barrier(probabilities.astype(jnp.bfloat16))
    blended = jnp.einsum('rkgt,rtkd->rkgd', rounded.astype(jnp.float32), value_rows.astype(jnp.float32))
    return (peak, weight_sum, blended)

def reference(query, key_cache, value_cache, new_key, new_value, lengths, out_weight, residual, norm_gain, expert_ids, gate_weights, w_gate, w_up, w_down):
    grouping = HEADS // KV_HEADS
    scaling = HD ** (-0.5)
    queries = query.reshape(REQUESTS, KV_HEADS, grouping, HD)
    key_rows = key_cache.reshape(REQUESTS, LEN, KV_HEADS, HD)
    value_rows = value_cache.reshape(REQUESTS, LEN, KV_HEADS, HD)
    position = jnp.arange(LEN, dtype=jnp.int32)
    visible = position[None, :] < lengths[:, None]
    softmax_state = block_softmax(queries, key_rows, value_rows, visible, scaling)
    fresh_key = new_key.reshape(REQUESTS, KV_HEADS, HD).astype(jnp.float32)
    fresh_value = new_value.reshape(REQUESTS, KV_HEADS, HD).astype(jnp.float32)
    own_score = jnp.einsum('rkgd,rkd->rkg', queries.astype(jnp.float32), fresh_key) * scaling
    own_state = (own_score, jnp.ones_like(own_score), jnp.broadcast_to(fresh_value[:, :, None, :], softmax_state[2].shape))
    softmax_state = merge_pair(softmax_state, own_state)
    attended = (softmax_state[2] / softmax_state[1][..., None]).reshape(REQUESTS, HEADS * HD).astype(jnp.bfloat16)
    projected = jnp.dot(attended, out_weight, preferred_element_type=jnp.float32)
    stream = residual.astype(jnp.float32) + projected
    normed = (stream * lax.rsqrt(lax.optimization_barrier(jnp.mean(stream * stream, axis=-1, keepdims=True)) + norm_epsilon) * norm_gain).astype(jnp.bfloat16)
    chosen = (expert_ids[:, :, None] == jnp.arange(EXPERTS, dtype=jnp.int32)).astype(jnp.float32)
    coefficients = lax.optimization_barrier(jnp.sum(chosen * gate_weights[:, :, None], axis=1))
    hidden_share = FF // N_TP

    def expert_step(running, inputs):
        gate_slice, up_slice, down_slice, column = inputs
        gate_act = jnp.dot(normed, gate_slice, preferred_element_type=jnp.float32)
        up_act = jnp.dot(normed, up_slice, preferred_element_type=jnp.float32)
        hidden = (jax.nn.silu(gate_act) * up_act).astype(jnp.bfloat16)
        hidden_parts = hidden.reshape(REQUESTS, N_TP, hidden_share).astype(jnp.float32)
        down_parts = down_slice.reshape(N_TP, hidden_share, D).astype(jnp.float32)
        partials = jnp.einsum('rpf,pfd->prd', hidden_parts, down_parts)
        rounded = lax.optimization_barrier(partials.astype(jnp.bfloat16))
        output = lax.optimization_barrier(jnp.sum(rounded.astype(jnp.float32), axis=0)).astype(jnp.bfloat16)
        return (running + column[:, None] * output.astype(jnp.float32), None)
    mixture, unused = lax.scan(expert_step, jnp.zeros((REQUESTS, D), jnp.float32), (w_gate, w_up, w_down, coefficients.T))
    return (stream + mixture).astype(jnp.bfloat16)
```

```python
import functools

import jax
import jax.numpy as jnp
from jax import lax
from jax.experimental import pallas as pl
from jax.experimental.pallas import tpu as pltpu
from jax.sharding import PartitionSpec as P

HEADS = 32
KV_HEADS = 4
HD = 128
TOP = 8
LANES = 128

masked_fill = -1e30
norm_epsilon = 1e-06
bf16 = jnp.bfloat16
f32 = jnp.float32


def attention_kernel(
    block_rows, kv_count, per_group, place_ref, lengths_ref, query_ref, key_ref, value_ref,
    new_key_ref, new_value_ref, out_ref, rows_ref
):
    step = pl.program_id(0)
    cached = key_ref.shape[1]
    heads = kv_count * per_group
    scaling = HD ** (-0.5)
    position = lax.broadcasted_iota(jnp.int32, (heads, cached), 1)
    scores, own = [], []
    for row in range(block_rows):
        queries = query_ref[row]
        score = lax.dot_general(
            queries, key_ref[row], (((1,), (1,)), ((), ())), preferred_element_type=f32
        )
        visible = position < lengths_ref[step * block_rows + row]
        scores.append(jnp.where(visible, score * scaling, masked_fill))
        fresh = new_key_ref[row].astype(f32)
        own.append(jnp.sum(queries.astype(f32) * fresh, axis=1, keepdims=True) * scaling)
    scores = jnp.concatenate(scores, axis=0)
    own = jnp.concatenate(own, axis=0)
    peak = jnp.maximum(jnp.max(scores, axis=1, keepdims=True), own)
    weights = jnp.exp(scores - peak)
    own_weight = jnp.exp(own - peak)
    total = jnp.sum(weights, axis=1, keepdims=True) + own_weight
    weights = weights.astype(bf16)
    inverse = 1.0 / total
    for row in range(block_rows):
        at = slice(row * heads, (row + 1) * heads)
        blended = jnp.dot(weights[at], value_ref[row], preferred_element_type=f32)
        fresh = new_value_ref[row].astype(f32)
        blended = (blended + own_weight[at] * fresh) * inverse[at]
        for kv in range(kv_count):
            rows_ref[step * block_rows + row, kv * per_group : (kv + 1) * per_group, :] = blended[
                kv * per_group : (kv + 1) * per_group, kv * HD : (kv + 1) * HD
            ]

    @pl.when(step == pl.num_programs(0) - 1)
    def _():
        for head in range(heads):
            out_ref[:, head * HD : (head + 1) * HD] = rows_ref[:, head, :].astype(bf16)


def attend(query, key_cache, value_cache, new_key, new_value, lengths, tp_index):
    rows, width = query.shape
    cached = key_cache.shape[1]
    heads = width // HD
    grouping = HEADS // KV_HEADS
    kv_count = max(1, heads // grouping)
    per_group = heads // kv_count
    kv_block = tp_index * heads // grouping // kv_count
    kv_width = kv_count * HD
    spread = query.reshape(rows, kv_count, per_group, 1, HD) * jnp.eye(kv_count, dtype=bf16)[
        None, :, None, :, None
    ]
    spread = spread.reshape(rows, heads, kv_width)
    fresh_key = lax.dynamic_slice_in_dim(new_key, kv_block * kv_width, kv_width, 1)
    fresh_value = lax.dynamic_slice_in_dim(new_value, kv_block * kv_width, kv_width, 1)
    block_rows = 4
    grid_spec = pltpu.PrefetchScalarGridSpec(
        num_scalar_prefetch=2,
        grid=(rows // block_rows,),
        in_specs=[
            pl.BlockSpec((block_rows, heads, kv_width), lambda i, place, lens: (i, 0, 0)),
            pl.BlockSpec((block_rows, cached, kv_width), lambda i, place, lens: (i, 0, place[0])),
            pl.BlockSpec((block_rows, cached, kv_width), lambda i, place, lens: (i, 0, place[0])),
            pl.BlockSpec((block_rows, 1, kv_width), lambda i, place, lens: (i, 0, 0)),
            pl.BlockSpec((block_rows, 1, kv_width), lambda i, place, lens: (i, 0, 0)),
        ],
        out_specs=pl.BlockSpec((rows, width), lambda i, place, lens: (0, 0)),
        scratch_shapes=[pltpu.VMEM((rows, heads, HD), f32)],
    )
    return pl.pallas_call(
        functools.partial(attention_kernel, block_rows, kv_count, per_group),
        grid_spec=grid_spec,
        out_shape=jax.ShapeDtypeStruct((rows, width), bf16),
        compiler_params=pltpu.CompilerParams(
            dimension_semantics=("arbitrary",), vmem_limit_bytes=16 * 2**20
        ),
        name="attention",
    )(
        kv_block.astype(jnp.int32).reshape(1),
        lengths,
        spread,
        key_cache,
        value_cache,
        fresh_key.reshape(rows, 1, kv_width),
        fresh_value.reshape(rows, 1, kv_width),
    )


def shift(array, axis, by):
    size = lax.axis_size(axis)
    return lax.ppermute(array, axis, [(i, (i + by) % size) for i in range(size)])


def shards(
    query,
    key_cache,
    value_cache,
    new_key,
    new_value,
    lengths,
    out_weight,
    residual,
    norm_gain,
    expert_ids,
    gate_weights,
    w_gate,
    w_up,
    w_down,
):
    rows = query.shape[0]
    width = residual.shape[1]
    n_ep, n_tp, n_sp = lax.axis_size("ep"), lax.axis_size("tp"), lax.axis_size("sp")
    ep_index, tp_index, sp_index = (lax.axis_index(name) for name in ("ep", "tp", "sp"))
    local_experts = w_gate.shape[0]
    experts = local_experts * n_ep * n_sp
    half = width // n_sp
    part = rows // n_tp
    out_width = width // n_tp

    chosen = expert_ids[:, :, None] == jnp.arange(experts, dtype=jnp.int32)
    coefficients = jnp.sum(jnp.where(chosen, gate_weights[:, :, None], 0.0), axis=1)
    high = lax.reduce_precision(coefficients, 8, 7)
    coefficients = jnp.concatenate(
        [high.astype(bf16), (coefficients - high).astype(bf16)], axis=1
    )
    coefficients = jnp.pad(coefficients, ((0, 0), (0, -2 * experts % LANES)))

    attended = attend(query, key_cache, value_cache, new_key, new_value, lengths, tp_index)

    residual_sent = lax.dynamic_slice_in_dim(residual, (1 - sp_index) * half, half, 1)
    packed = jnp.concatenate([attended, residual_sent, coefficients], axis=1)
    packed_other = shift(packed, "sp", 1)
    both = jnp.stack([attended, packed_other[:, : attended.shape[1]]])
    residual_both = jnp.stack(
        [
            lax.dynamic_slice_in_dim(residual, sp_index * half, half, 1),
            packed_other[:, attended.shape[1] : attended.shape[1] + half],
        ]
    )
    coefficients_both = jnp.stack([coefficients, packed_other[:, attended.shape[1] + half :]])
    terms = jnp.dot(
        both.reshape(2 * rows, -1), out_weight, preferred_element_type=f32
    ).reshape(2, n_tp, part, half)

    def block_of(array, index):
        return lax.dynamic_slice_in_dim(array, index % n_tp, 1, 1)[:, 0]

    stream = block_of(terms, tp_index) + block_of(
        residual_both.reshape(2, n_tp, part, half), tp_index
    ).astype(f32)
    for by in range(1, n_tp):
        stream = stream + shift(block_of(terms, tp_index + by).astype(bf16), "tp", by).astype(f32)
    own_coefficients = block_of(coefficients_both.reshape(2, n_tp, part, -1), tp_index)
    piece = jnp.concatenate([stream.astype(bf16), own_coefficients], axis=2)

    along_ep = jnp.stack([piece] + [shift(piece, "ep", by) for by in range(1, n_ep)])
    along_tp = jnp.stack(
        [along_ep] + [shift(along_ep, "tp", by) for by in range(1, n_tp)], axis=1
    )
    other = shift(along_tp[..., :half], "sp", 1)[:, :, ::-1]
    mine = along_tp[..., :half]
    streams = jnp.where(
        sp_index == 0,
        jnp.concatenate([mine, other], axis=4),
        jnp.concatenate([other, mine], axis=4),
    )
    streams = streams.reshape(-1, width)
    values = streams.astype(f32)
    normed = (
        values
        * lax.rsqrt(jnp.mean(values * values, axis=-1, keepdims=True) + norm_epsilon)
        * norm_gain
    ).astype(bf16)
    table = along_tp[..., half:].reshape(streams.shape[0], -1).astype(f32)
    first_expert = (ep_index * n_sp + sp_index) * local_experts
    mixture = 0.0
    for expert in range(local_experts):
        gate_act = jnp.dot(normed, w_gate[expert], preferred_element_type=f32)
        up_act = jnp.dot(normed, w_up[expert], preferred_element_type=f32)
        hidden = (jax.nn.silu(gate_act) * up_act).astype(bf16)
        down = jnp.dot(hidden, w_down[expert], preferred_element_type=f32)
        at = first_expert + expert
        scale = lax.dynamic_slice_in_dim(table, at, 1, 1) + lax.dynamic_slice_in_dim(
            table, at + experts, 1, 1
        )
        mixture = mixture + scale * down

    mixture = mixture.reshape(n_ep, n_tp, 2, part, width)
    mixture = mixture[:, :, 0] + shift(mixture[:, :, 1].astype(bf16), "sp", 1).astype(f32)

    def columns_of(array, index):
        return lax.dynamic_slice_in_dim(array, index % n_tp * out_width, out_width, array.ndim - 1)

    total = columns_of(mixture, tp_index)
    for by in range(1, n_tp):
        arrived = shift(columns_of(mixture, tp_index + by).astype(bf16), "tp", by)
        total = total + jnp.roll(arrived, by, axis=1).astype(f32)
    final = total[0]
    for by in range(1, n_ep):
        final = final + shift(total[by].astype(bf16), "ep", -by).astype(f32)
    own_stream = columns_of(streams.reshape(n_ep, n_tp, 2, part, width)[0, :, 0], tp_index)
    final = (final + own_stream.astype(f32)).astype(bf16)
    order = (tp_index - jnp.arange(n_tp)) % n_tp
    return jnp.take(final, order, axis=0).reshape(rows, out_width)


def solution(mesh):
    placed = (
        P(("groups", "ep", "sp"), "tp"),
        P(("groups", "ep", "sp"), None, None),
        P(("groups", "ep", "sp"), None, None),
        P(("groups", "ep", "sp"), None),
        P(("groups", "ep", "sp"), None),
        P(("groups", "ep", "sp")),
        P("tp", "sp"),
        P(("groups", "ep", "sp"), None),
        P(),
        P(("groups", "ep", "sp"), None),
        P(("groups", "ep", "sp"), None),
        P(("ep", "sp"), None, "tp"),
        P(("ep", "sp"), None, "tp"),
        P(("ep", "sp"), "tp", None),
    )
    return jax.shard_map(
        shards,
        mesh=mesh,
        in_specs=placed,
        out_specs=P(("groups", "ep", "sp"), "tp"),
        check_vma=False,
    )
```

```python
import functools

import jax
import jax.numpy as jnp
from jax import lax
from jax.experimental import pallas as pl
from jax.experimental.pallas import tpu as pltpu
from jax.sharding import PartitionSpec as P

HEADS = 32
KV_HEADS = 4
HD = 128
LANES = 128
MIB = 2**20

masked_fill = -1e30
norm_epsilon = 1e-06
bf16 = jnp.bfloat16
f32 = jnp.float32


def attention_kernel(
    kv_count, per_group, chunk, experts, kv_block_of, lengths_hbm, query_hbm, key_hbm, value_hbm,
    new_key_hbm, new_value_hbm, residual_hbm, ids_hbm, gates_hbm, weight_hbm,
    packed_ref, base_ref, weight_ref,
    query_ref, key_ref, value_ref, new_key_ref, new_value_ref, residual_ref, ids_ref, gates_ref,
    rows_ref, lengths_ref, small_sems, cache_sems, weight_sem,
):
    rows, cached, kv_width = key_ref.shape
    heads = kv_count * per_group
    half = base_ref.shape[1]
    chunks = rows // chunk
    kv_at = pl.multiple_of(kv_block_of(lax.axis_index("tp")) * kv_width, HD)
    sp_index = lax.axis_index("sp")
    kv_cols = pl.ds(kv_at, kv_width)
    small = [
        pltpu.make_async_copy(source, target, small_sems.at[i])
        for i, (source, target) in enumerate(
            [
                (query_hbm, query_ref),
                (new_key_hbm.at[:, kv_cols], new_key_ref),
                (new_value_hbm.at[:, kv_cols], new_value_ref),
                (lengths_hbm, lengths_ref),
                (residual_hbm, residual_ref),
                (ids_hbm, ids_ref),
                (gates_hbm, gates_ref),
            ]
        )
    ]
    for copy in small[:4]:
        copy.start()
    cache_copies = []
    for i in range(chunks):
        at = pl.ds(i * chunk, chunk)
        pair = [
            pltpu.make_async_copy(
                source.at[at, :, kv_cols], target.at[at], cache_sems.at[which, i]
            )
            for which, (source, target) in enumerate(
                [(key_hbm, key_ref), (value_hbm, value_ref)]
            )
        ]
        for copy in pair:
            copy.start()
        cache_copies.append(pair)
    for copy in small[4:]:
        copy.start()
    weight_copy = pltpu.make_async_copy(weight_hbm, weight_ref, weight_sem)
    weight_copy.start()
    for copy in small[:4]:
        copy.wait()

    scaling = HD ** (-0.5)
    position = lax.broadcasted_iota(jnp.int32, (heads, cached), 1)
    for head in range(heads):
        kv, group = head // per_group, head % per_group
        rows_ref[kv, pl.ds(group, rows, stride=per_group), :] = query_ref[
            :, head * HD : (head + 1) * HD
        ].astype(f32)
    blank = jnp.zeros((per_group, HD), f32)
    for i in range(chunks):
        cache_copies[i][0].wait()
        scores, own = [], []
        for row in range(i * chunk, (i + 1) * chunk):
            at = slice(row * per_group, (row + 1) * per_group)
            queries = jnp.concatenate(
                [
                    jnp.concatenate(
                        [rows_ref[kv, at, :] if kv == other else blank for other in range(kv_count)],
                        axis=1,
                    )
                    for kv in range(kv_count)
                ],
                axis=0,
            )
            score = lax.dot_general(
                queries.astype(bf16),
                key_ref[row],
                (((1,), (1,)), ((), ())),
                preferred_element_type=f32,
            )
            visible = position < lengths_ref[row]
            scores.append(jnp.where(visible, score * scaling, masked_fill))
            fresh = new_key_ref[row : row + 1, :].astype(f32)
            own.append(jnp.sum(queries * fresh, axis=1, keepdims=True) * scaling)
        scores = jnp.concatenate(scores, axis=0)
        own = jnp.concatenate(own, axis=0)
        peak = jnp.maximum(jnp.max(scores, axis=1, keepdims=True), own)
        weights = jnp.exp(scores - peak)
        own_weight = jnp.exp(own - peak)
        inverse = 1.0 / (jnp.sum(weights, axis=1, keepdims=True) + own_weight)
        weights = weights.astype(bf16)
        cache_copies[i][1].wait()
        for row in range(i * chunk, (i + 1) * chunk):
            at = slice((row - i * chunk) * heads, (row - i * chunk + 1) * heads)
            blended = jnp.dot(weights[at], value_ref[row], preferred_element_type=f32)
            fresh = new_value_ref[row : row + 1, :].astype(f32)
            blended = (blended + own_weight[at] * fresh) * inverse[at]
            for kv in range(kv_count):
                rows_ref[kv, row * per_group : (row + 1) * per_group, :] = blended[
                    kv * per_group : (kv + 1) * per_group, kv * HD : (kv + 1) * HD
                ]
    for copy in small[4:]:
        copy.wait()
    width = heads * HD
    for head in range(heads):
        kv, group = head // per_group, head % per_group
        packed_ref[:, head * HD : (head + 1) * HD] = rows_ref[
            kv, pl.ds(group, rows, stride=per_group), :
        ].astype(bf16)
    packed_ref[:, width : width + half] = residual_ref[
        :, pl.ds(pl.multiple_of((1 - sp_index) * half, LANES), half)
    ]
    base_ref[...] = residual_ref[:, pl.ds(pl.multiple_of(sp_index * half, LANES), half)]
    spare = packed_ref.shape[1] - width - half
    place = lax.broadcasted_iota(jnp.int32, (spare, rows), 0)
    expert = jnp.where(place < experts, place, place - experts)
    table = jnp.zeros((spare, rows), f32)
    for k in range(ids_ref.shape[0]):
        table = table + jnp.where(ids_ref[k : k + 1, :] == expert, gates_ref[k : k + 1, :], 0.0)
    high = table.astype(bf16).astype(f32)
    table = jnp.where(place < experts, high, table - high)
    packed_ref[:, width + half :] = table.T.astype(bf16)
    weight_copy.wait()


def in_hbm(array):
    return pltpu.with_memory_space_constraint(array, pltpu.HBM)


def in_vmem(array):
    return pltpu.with_memory_space_constraint(array, pltpu.VMEM)


ANYWHERE = pl.BlockSpec(memory_space=pl.ANY)
WHOLE = pl.BlockSpec(memory_space=pltpu.VMEM)


def attend(
    query, key_cache, value_cache, new_key, new_value, lengths, residual, expert_ids,
    gate_weights, out_weight, experts, n_sp
):
    rows, width = query.shape
    cached = key_cache.shape[1]
    heads = width // HD
    grouping = HEADS // KV_HEADS
    kv_count = max(1, heads // grouping)
    per_group = heads // kv_count
    kv_width = kv_count * HD

    def kv_block_of(tp_index):
        return tp_index * heads // grouping // kv_count

    half = residual.shape[1] // n_sp
    spare = -(-2 * experts // LANES) * LANES
    chunk = min(16, rows)
    arrays = [
        lengths, query, key_cache, value_cache, new_key, new_value, residual, expert_ids.T,
        gate_weights.T, out_weight
    ]
    return pl.pallas_call(
        functools.partial(attention_kernel, kv_count, per_group, chunk, experts, kv_block_of),
        in_specs=[ANYWHERE] * len(arrays),
        out_specs=[WHOLE] * 3,
        out_shape=[
            pltpu.VMEM((rows, width + half + spare), bf16),
            pltpu.VMEM((rows, half), bf16),
            pltpu.VMEM(out_weight.shape, bf16),
        ],
        scratch_shapes=[
            pltpu.VMEM((rows, width), bf16),
            pltpu.VMEM((rows, cached, kv_width), bf16),
            pltpu.VMEM((rows, cached, kv_width), bf16),
            pltpu.VMEM((rows, kv_width), bf16),
            pltpu.VMEM((rows, kv_width), bf16),
            pltpu.VMEM(residual.shape, bf16),
            pltpu.VMEM((expert_ids.shape[1], rows), jnp.int32),
            pltpu.VMEM((expert_ids.shape[1], rows), f32),
            pltpu.VMEM((kv_count, rows * per_group, HD), f32),
            pltpu.SMEM((rows,), jnp.int32),
            pltpu.SemaphoreType.DMA((7,)),
            pltpu.SemaphoreType.DMA((2, rows // chunk)),
            pltpu.SemaphoreType.DMA,
        ],
        compiler_params=pltpu.CompilerParams(vmem_limit_bytes=24 * MIB),
        name="attention",
    )(*map(in_hbm, arrays))


def project_kernel(width, packed_ref, other_ref, weight_ref, terms_ref, sent_ref):
    both = jnp.concatenate([packed_ref[:, :width], other_ref[:, :width]], axis=0)
    terms = jnp.dot(both, weight_ref[...], preferred_element_type=f32)
    terms_ref[...] = terms
    sent_ref[...] = terms.astype(bf16)


def project(packed, packed_other, weight):
    shape = (2 * packed.shape[0], weight.shape[1])
    return pl.pallas_call(
        functools.partial(project_kernel, weight.shape[0]),
        in_specs=[WHOLE] * 3,
        out_specs=[WHOLE] * 2,
        out_shape=[pltpu.VMEM(shape, f32), pltpu.VMEM(shape, bf16)],
        compiler_params=pltpu.CompilerParams(vmem_limit_bytes=8 * MIB),
        name="project",
    )(in_vmem(packed), in_vmem(packed_other), in_vmem(weight))


def load_kernel(*refs):
    *arrays, sems = refs
    count = len(arrays) // 2
    copies = [
        pltpu.make_async_copy(arrays[i], arrays[count + i], sems.at[i]) for i in range(count)
    ]
    for copy in copies:
        copy.start()
    for copy in copies:
        copy.wait()


def load(*arrays):
    return pl.pallas_call(
        load_kernel,
        in_specs=[ANYWHERE] * len(arrays),
        out_specs=[WHOLE] * len(arrays),
        out_shape=[pltpu.VMEM(array.shape, array.dtype) for array in arrays],
        scratch_shapes=[pltpu.SemaphoreType.DMA((len(arrays),))],
        compiler_params=pltpu.CompilerParams(vmem_limit_bytes=16 * MIB),
        cost_estimate=pl.CostEstimate(
            flops=0, bytes_accessed=2 * sum(array.nbytes for array in arrays), transcendentals=0
        ),
        name="load_weights",
    )(*map(in_hbm, arrays))


def experts_kernel(experts, first_of, places, *refs):
    count = len(places)
    mine, other = refs[:count], refs[count : 2 * count]
    gain_ref, gate_ref, up_ref, down_ref, keep_ref, send_ref, rows_ref, table_ref = refs[2 * count :]
    half = rows_ref.shape[1] // 2
    rows = rows_ref.shape[0]
    sp_index = lax.axis_index("sp")
    tp_index = lax.axis_index("tp")
    my_cols = pl.ds(pl.multiple_of(sp_index * half, LANES), half)
    other_cols = pl.ds(pl.multiple_of((1 - sp_index) * half, LANES), half)
    for a, b, (start, step, flip) in zip(mine, other, places):
        m = a.shape[0] // 2
        at = start if flip is None else pl.multiple_of(start + (tp_index ^ flip) * step, step)
        first, second = pl.ds(at, m), pl.ds(rows // 2 + at, m)
        rows_ref[first, my_cols] = a[:m, :half]
        rows_ref[second, my_cols] = a[m:, :half]
        rows_ref[first, other_cols] = b[m:, :half]
        rows_ref[second, other_cols] = b[:m, :half]
        table_ref[first, :] = a[:m, half:].astype(f32)
        table_ref[second, :] = a[m:, half:].astype(f32)
    values = rows_ref[...].astype(f32)
    inverse = lax.rsqrt(jnp.mean(values * values, axis=1, keepdims=True) + norm_epsilon)
    rows_ref[...] = (values * inverse * gain_ref[...]).astype(bf16)
    first_expert = first_of(lax.axis_index("ep"), sp_index)
    table = table_ref[...]
    lane = lax.broadcasted_iota(jnp.int32, table.shape, 1)
    total = None
    for e in range(gate_ref.shape[0]):
        wanted = (lane == first_expert + e) | (lane == first_expert + e + experts)
        scale = jnp.sum(jnp.where(wanted, table, 0.0), axis=1, keepdims=True)
        normed = rows_ref[...]
        gate = jnp.dot(normed, gate_ref[e], preferred_element_type=f32)
        up = jnp.dot(normed, up_ref[e], preferred_element_type=f32)
        hidden = (gate / (1.0 + jnp.exp(-gate)) * up * scale).astype(bf16)
        term = jnp.dot(hidden, down_ref[e], preferred_element_type=f32)
        total = term if total is None else total + term
    keep_ref[...] = total[: rows // 2]
    send_ref[...] = total[rows // 2 :].astype(bf16)


def run_experts(mine, other, places, gain, gate, up, down, experts, n_sp):
    rows = sum(array.shape[0] for array in mine)
    width = gain.shape[0]
    local = gate.shape[0]
    arrays = [*mine, *other, gain.reshape(1, width), gate, up, down]
    return pl.pallas_call(
        functools.partial(experts_kernel, experts, lambda e, s: (e * n_sp + s) * local, places),
        in_specs=[WHOLE] * len(arrays),
        out_specs=[WHOLE] * 2,
        out_shape=[pltpu.VMEM((rows // 2, width), f32), pltpu.VMEM((rows // 2, width), bf16)],
        scratch_shapes=[
            pltpu.VMEM((rows, width), bf16),
            pltpu.VMEM((rows, mine[0].shape[1] - width // 2), f32),
        ],
        compiler_params=pltpu.CompilerParams(vmem_limit_bytes=(24 if rows <= 256 else 48) * MIB),
        name="experts",
    )(*[array if array.shape[0] == 1 else in_vmem(array) for array in arrays])


def swap(array, axis, by=1):
    size = lax.axis_size(axis)
    return lax.ppermute(array, axis, [(i, i ^ by) for i in range(size)])


def shards(
    query,
    key_cache,
    value_cache,
    new_key,
    new_value,
    lengths,
    out_weight,
    residual,
    norm_gain,
    expert_ids,
    gate_weights,
    w_gate,
    w_up,
    w_down,
):
    rows = query.shape[0]
    width = residual.shape[1]
    n_ep, n_tp, n_sp = lax.axis_size("ep"), lax.axis_size("tp"), lax.axis_size("sp")
    tp_index, sp_index = lax.axis_index("tp"), lax.axis_index("sp")
    experts = w_gate.shape[0] * n_ep * n_sp
    half = width // n_sp
    part = rows // n_tp
    out_width = width // n_tp
    heads_width = query.shape[1]

    packed, base, weight = attend(
        query, key_cache, value_cache, new_key, new_value, lengths, residual, expert_ids,
        gate_weights, out_weight, experts, n_sp
    )
    packed_other = swap(packed, "sp")
    terms, sent = project(packed, packed_other, weight)
    totals = terms
    for by in range(1, n_tp):
        totals = totals + swap(sent, "tp", by).astype(f32)
    residual_both = jnp.concatenate([base, packed_other[:, heads_width : heads_width + half]], axis=0)
    table = jnp.concatenate([packed[:, heads_width + half :], packed_other[:, heads_width + half :]], axis=0)
    stream = (totals + residual_both.astype(f32)).astype(bf16)
    chip = jnp.concatenate([stream, table], axis=1)
    piece = lax.dynamic_slice_in_dim(
        chip.reshape(2, n_tp, part, -1), tp_index, 1, 1
    ).reshape(2 * part, -1)

    mine, places = [chip], [(0, rows, None)]
    for by in range(1, n_ep):
        arrived = swap(piece, "ep", by)
        for flip in range(n_tp):
            mine.append(swap(arrived, "tp", flip) if flip else arrived)
            places.append((by * rows, part, flip))
    w_gate, w_up, w_down, _ = lax.optimization_barrier((w_gate, w_up, w_down, piece))
    w_gate, w_up, w_down = load(w_gate, w_up, w_down)
    if part % 16:
        blocks = jnp.stack(mine[1:]).reshape(n_ep - 1, n_tp, 2, part, -1)
        bit = 1
        while bit < n_tp:
            flipped = blocks[:, jnp.array([j ^ bit for j in range(n_tp)])]
            blocks = jnp.where(tp_index & bit, flipped, blocks)
            bit *= 2
        blocks = blocks.transpose(2, 0, 1, 3, 4).reshape(2, (n_ep - 1) * rows, -1)
        mine = [jnp.concatenate([chip.reshape(2, rows, -1), blocks], axis=1).reshape(2 * n_ep * rows, -1)]
        places = [(0, rows, None)]
    other = [swap(array, "sp") for array in mine]
    keep, send = run_experts(
        mine, other, tuple(places), norm_gain, w_gate, w_up, w_down, experts, n_sp
    )
    mixture = (keep + swap(send, "sp").astype(f32)).reshape(n_ep, rows, width)

    def columns_of(array, index):
        return lax.dynamic_slice_in_dim(array, index * out_width, out_width, array.ndim - 1)

    total = columns_of(mixture, tp_index)
    for by in range(1, n_tp):
        total = total + swap(columns_of(mixture, tp_index ^ by).astype(bf16), "tp", by).astype(f32)
    final = total[0]
    for by in range(1, n_ep):
        final = final + swap(total[by].astype(bf16), "ep", by).astype(f32)

    start = tp_index * out_width - sp_index * half
    local = lax.dynamic_slice_in_dim(totals[:rows], jnp.clip(start, 0, half - out_width), out_width, 1)
    aside = jnp.clip(tp_index * out_width - sp_index * half, 0, half - out_width)
    arrived = swap(lax.dynamic_slice_in_dim(totals[rows:], aside, out_width, 1).astype(bf16), "sp")
    here = tp_index * out_width // half == sp_index
    projected = jnp.where(here, local, arrived.astype(f32))
    return (final + (projected + columns_of(residual, tp_index).astype(f32))).astype(bf16)


def solution(mesh):
    placed = (
        P(("groups", "ep", "sp"), "tp"),
        P(("groups", "ep", "sp"), None, None),
        P(("groups", "ep", "sp"), None, None),
        P(("groups", "ep", "sp"), None),
        P(("groups", "ep", "sp"), None),
        P(("groups", "ep", "sp")),
        P("tp", "sp"),
        P(("groups", "ep", "sp"), None),
        P(),
        P(("groups", "ep", "sp"), None),
        P(("groups", "ep", "sp"), None),
        P(("ep", "sp"), None, "tp"),
        P(("ep", "sp"), None, "tp"),
        P(("ep", "sp"), "tp", None),
    )
    return jax.shard_map(
        shards,
        mesh=mesh,
        in_specs=placed,
        out_specs=P(("groups", "ep", "sp"), "tp"),
        check_vma=False,
    )
```

```python
import functools

import jax
import jax.numpy as jnp
from jax import lax
from jax.experimental import pallas as pl
from jax.experimental.pallas import tpu as pltpu
from jax.sharding import PartitionSpec as P

HEADS = 32
KV_HEADS = 4
HD = 128
LANES = 128
MIB = 2**20

masked_fill = -1e30
norm_epsilon = 1e-06
bf16 = jnp.bfloat16
f32 = jnp.float32


def attention_kernel(
    kv_count, per_group, chunk, experts, kv_block_of, lengths_hbm, query_hbm, key_hbm, value_hbm,
    new_key_hbm, new_value_hbm, residual_hbm, ids_hbm, gates_hbm, weight_hbm,
    packed_ref, base_ref, weight_ref,
    query_ref, key_ref, value_ref, new_key_ref, new_value_ref, residual_ref, ids_ref, gates_ref,
    rows_ref, lengths_ref, small_sems, cache_sems, weight_sem,
):
    rows, cached, kv_width = key_ref.shape
    heads = kv_count * per_group
    half = base_ref.shape[1]
    chunks = rows // chunk
    kv_at = pl.multiple_of(kv_block_of(lax.axis_index("tp")) * kv_width, HD)
    sp_index = lax.axis_index("sp")
    kv_cols = pl.ds(kv_at, kv_width)
    small = [
        pltpu.make_async_copy(source, target, small_sems.at[i])
        for i, (source, target) in enumerate(
            [
                (query_hbm, query_ref),
                (new_key_hbm.at[:, kv_cols], new_key_ref),
                (new_value_hbm.at[:, kv_cols], new_value_ref),
                (lengths_hbm, lengths_ref),
                (residual_hbm, residual_ref),
                (ids_hbm, ids_ref),
                (gates_hbm, gates_ref),
            ]
        )
    ]
    for copy in small[:4]:
        copy.start()
    cache_copies = []
    for i in range(chunks):
        at = pl.ds(i * chunk, chunk)
        pair = [
            pltpu.make_async_copy(
                source.at[at, :, kv_cols], target.at[at], cache_sems.at[which, i]
            )
            for which, (source, target) in enumerate(
                [(key_hbm, key_ref), (value_hbm, value_ref)]
            )
        ]
        for copy in pair:
            copy.start()
        cache_copies.append(pair)
    for copy in small[4:]:
        copy.start()
    weight_copy = pltpu.make_async_copy(weight_hbm, weight_ref, weight_sem)
    weight_copy.start()
    for copy in small[:4]:
        copy.wait()

    scaling = HD ** (-0.5)
    position = lax.broadcasted_iota(jnp.int32, (heads, cached), 1)
    for head in range(heads):
        kv, group = head // per_group, head % per_group
        rows_ref[kv, pl.ds(group, rows, stride=per_group), :] = query_ref[
            :, head * HD : (head + 1) * HD
        ].astype(f32)
    blank = jnp.zeros((per_group, HD), f32)
    for i in range(chunks):
        cache_copies[i][0].wait()
        scores, own = [], []
        for row in range(i * chunk, (i + 1) * chunk):
            at = slice(row * per_group, (row + 1) * per_group)
            queries = jnp.concatenate(
                [
                    jnp.concatenate(
                        [rows_ref[kv, at, :] if kv == other else blank for other in range(kv_count)],
                        axis=1,
                    )
                    for kv in range(kv_count)
                ],
                axis=0,
            )
            score = lax.dot_general(
                queries.astype(bf16),
                key_ref[row],
                (((1,), (1,)), ((), ())),
                preferred_element_type=f32,
            )
            visible = position < lengths_ref[row]
            scores.append(jnp.where(visible, score * scaling, masked_fill))
            fresh = new_key_ref[row : row + 1, :].astype(f32)
            own.append(jnp.sum(queries * fresh, axis=1, keepdims=True) * scaling)
        scores = jnp.concatenate(scores, axis=0)
        own = jnp.concatenate(own, axis=0)
        peak = jnp.maximum(jnp.max(scores, axis=1, keepdims=True), own)
        weights = jnp.exp(scores - peak)
        own_weight = jnp.exp(own - peak)
        inverse = 1.0 / (jnp.sum(weights, axis=1, keepdims=True) + own_weight)
        weights = weights.astype(bf16)
        cache_copies[i][1].wait()
        for row in range(i * chunk, (i + 1) * chunk):
            at = slice((row - i * chunk) * heads, (row - i * chunk + 1) * heads)
            blended = jnp.dot(weights[at], value_ref[row], preferred_element_type=f32)
            fresh = new_value_ref[row : row + 1, :].astype(f32)
            blended = (blended + own_weight[at] * fresh) * inverse[at]
            for kv in range(kv_count):
                rows_ref[kv, row * per_group : (row + 1) * per_group, :] = blended[
                    kv * per_group : (kv + 1) * per_group, kv * HD : (kv + 1) * HD
                ]
    for copy in small[4:]:
        copy.wait()
    width = heads * HD
    for head in range(heads):
        kv, group = head // per_group, head % per_group
        packed_ref[:, head * HD : (head + 1) * HD] = rows_ref[
            kv, pl.ds(group, rows, stride=per_group), :
        ].astype(bf16)
    packed_ref[:, width : width + half] = residual_ref[
        :, pl.ds(pl.multiple_of((1 - sp_index) * half, LANES), half)
    ]
    base_ref[...] = residual_ref[:, pl.ds(pl.multiple_of(sp_index * half, LANES), half)]
    spare = packed_ref.shape[1] - width - half
    place = lax.broadcasted_iota(jnp.int32, (spare, rows), 0)
    expert = jnp.where(place < experts, place, place - experts)
    table = jnp.zeros((spare, rows), f32)
    for k in range(ids_ref.shape[0]):
        table = table + jnp.where(ids_ref[k : k + 1, :] == expert, gates_ref[k : k + 1, :], 0.0)
    high = table.astype(bf16).astype(f32)
    table = jnp.where(place < experts, high, table - high)
    packed_ref[:, width + half :] = table.T.astype(bf16)
    weight_copy.wait()


def in_hbm(array):
    return pltpu.with_memory_space_constraint(array, pltpu.HBM)


def in_vmem(array):
    return pltpu.with_memory_space_constraint(array, pltpu.VMEM)


FREE = pl.CostEstimate(flops=0, bytes_accessed=0, transcendentals=0)
ANYWHERE = pl.BlockSpec(memory_space=pl.ANY)
WHOLE = pl.BlockSpec(memory_space=pltpu.VMEM)


def attend(
    query, key_cache, value_cache, new_key, new_value, lengths, residual, expert_ids,
    gate_weights, out_weight, experts, n_sp
):
    rows, width = query.shape
    cached = key_cache.shape[1]
    heads = width // HD
    grouping = HEADS // KV_HEADS
    kv_count = max(1, heads // grouping)
    per_group = heads // kv_count
    kv_width = kv_count * HD

    def kv_block_of(tp_index):
        return tp_index * heads // grouping // kv_count

    half = residual.shape[1] // n_sp
    spare = -(-2 * experts // LANES) * LANES
    chunk = min(16, rows)
    arrays = [
        lengths, query, key_cache, value_cache, new_key, new_value, residual, expert_ids.T,
        gate_weights.T, out_weight
    ]
    return pl.pallas_call(
        functools.partial(attention_kernel, kv_count, per_group, chunk, experts, kv_block_of),
        in_specs=[ANYWHERE] * len(arrays),
        out_specs=[WHOLE] * 3,
        out_shape=[
            pltpu.VMEM((rows, width + half + spare), bf16),
            pltpu.VMEM((rows, half), bf16),
            pltpu.VMEM(out_weight.shape, bf16),
        ],
        scratch_shapes=[
            pltpu.VMEM((rows, width), bf16),
            pltpu.VMEM((rows, cached, kv_width), bf16),
            pltpu.VMEM((rows, cached, kv_width), bf16),
            pltpu.VMEM((rows, kv_width), bf16),
            pltpu.VMEM((rows, kv_width), bf16),
            pltpu.VMEM(residual.shape, bf16),
            pltpu.VMEM((expert_ids.shape[1], rows), jnp.int32),
            pltpu.VMEM((expert_ids.shape[1], rows), f32),
            pltpu.VMEM((kv_count, rows * per_group, HD), f32),
            pltpu.SMEM((rows,), jnp.int32),
            pltpu.SemaphoreType.DMA((7,)),
            pltpu.SemaphoreType.DMA((2, rows // chunk)),
            pltpu.SemaphoreType.DMA,
        ],
        compiler_params=pltpu.CompilerParams(vmem_limit_bytes=24 * MIB),
        cost_estimate=FREE,
        name="attention",
    )(*map(in_hbm, arrays))


def project_kernel(
    packed_ref, other_ref, base_ref, weight_ref, send_first, send_last, keep_first, keep_last,
    table_first, table_last, terms_ref
):
    rows, half = base_ref.shape
    width = weight_ref.shape[0]
    part = rows // 2
    tp_index = lax.axis_index("tp")
    both = jnp.concatenate([packed_ref[:, :width], other_ref[:, :width]], axis=0)
    terms_ref[...] = jnp.dot(both, weight_ref[...], preferred_element_type=f32)
    for block, send_ref, keep_ref, table_ref in (
        (tp_index, send_last, keep_first, table_first),
        (1 - tp_index, send_first, keep_last, table_last),
    ):
        own = pl.ds(pl.multiple_of(block * part, part), part)
        for i, residual in enumerate((base_ref[own, :], other_ref[own, width : width + half])):
            to = slice(i * part, (i + 1) * part)
            terms = terms_ref[pl.ds(pl.multiple_of(i * rows + block * part, part), part), :]
            send_ref[to, :] = terms.astype(bf16)
            keep_ref[to, :] = terms + residual.astype(f32)
        table_ref[:part, :] = packed_ref[own, width + half :]
        table_ref[part:, :] = other_ref[own, width + half :]


def project(packed, packed_other, base, weight):
    shape = base.shape
    table = (shape[0], packed.shape[1] - weight.shape[0] - shape[1])
    return pl.pallas_call(
        project_kernel,
        in_specs=[WHOLE] * 4,
        out_specs=[WHOLE] * 6,
        out_shape=[
            *[pltpu.VMEM(shape, bf16)] * 2,
            *[pltpu.VMEM(shape, f32)] * 2,
            *[pltpu.VMEM(table, bf16)] * 2,
        ],
        scratch_shapes=[pltpu.VMEM((2 * shape[0], shape[1]), f32)],
        compiler_params=pltpu.CompilerParams(vmem_limit_bytes=8 * MIB),
        cost_estimate=FREE,
        name="project",
    )(*map(in_vmem, (packed, packed_other, base, weight)))


def load_kernel(*refs):
    *arrays, sems = refs
    count = len(arrays) // 2
    copies = [
        pltpu.make_async_copy(arrays[i], arrays[count + i], sems.at[i]) for i in range(count)
    ]
    for copy in copies:
        copy.start()
    for copy in copies:
        copy.wait()


def load(*arrays):
    return pl.pallas_call(
        load_kernel,
        in_specs=[ANYWHERE] * len(arrays),
        out_specs=[WHOLE] * len(arrays),
        out_shape=[pltpu.VMEM(array.shape, array.dtype) for array in arrays],
        scratch_shapes=[pltpu.SemaphoreType.DMA((len(arrays),))],
        compiler_params=pltpu.CompilerParams(vmem_limit_bytes=16 * MIB),
        cost_estimate=pl.CostEstimate(
            flops=0, bytes_accessed=0, transcendentals=0
        ),
        name="load_weights",
    )(*map(in_hbm, arrays))


def experts_kernel(experts, first_of, places, streams, loads, *refs):
    count = len(places)
    mine, other = refs[:count], refs[count : 2 * count]
    gain_ref, gate_ref, up_ref, down_ref, keep_ref, send_ref, *refs = refs[2 * count :]
    stream_ref = refs.pop(0) if streams else None
    if loads:
        down_hbm, down_ref, rows_ref, table_ref, sem = down_ref, *refs
        down_copy = pltpu.make_async_copy(down_hbm, down_ref, sem)
        down_copy.start()
    else:
        rows_ref, table_ref = refs
    half = rows_ref.shape[1] // 2
    rows = rows_ref.shape[0]
    sp_index = lax.axis_index("sp")
    tp_index = lax.axis_index("tp")
    my_cols = pl.ds(pl.multiple_of(sp_index * half, LANES), half)
    other_cols = pl.ds(pl.multiple_of((1 - sp_index) * half, LANES), half)
    for a, b, segments in zip(mine, other, places):
        for source, m, start, flip in segments:
            at = start if flip is None else pl.multiple_of(start + (tp_index ^ flip) * m, m)
            own, others = pl.ds(at, m), pl.ds(rows // 2 + at, m)
            upper, lower = slice(source, source + m), slice(source + m, source + 2 * m)
            rows_ref[own, my_cols] = a[upper, :half]
            rows_ref[others, my_cols] = a[lower, :half]
            rows_ref[own, other_cols] = b[lower, :half]
            rows_ref[others, other_cols] = b[upper, :half]
            table_ref[own, :] = a[upper, half:].astype(f32)
            table_ref[others, :] = a[lower, half:].astype(f32)
    if streams:
        count, width = stream_ref.shape
        out_cols = pl.ds(pl.multiple_of(tp_index * width, LANES), width)
        stream_ref[...] = rows_ref[:count, out_cols]
    values = rows_ref[...].astype(f32)
    inverse = lax.rsqrt(jnp.mean(values * values, axis=1, keepdims=True) + norm_epsilon)
    rows_ref[...] = (values * inverse * gain_ref[...]).astype(bf16)
    first_expert = first_of(lax.axis_index("ep"), sp_index)
    table = table_ref[...]
    lane = lax.broadcasted_iota(jnp.int32, table.shape, 1)
    hidden = []
    for e in range(gate_ref.shape[0]):
        wanted = (lane == first_expert + e) | (lane == first_expert + e + experts)
        scale = jnp.sum(jnp.where(wanted, table, 0.0), axis=1, keepdims=True)
        normed = rows_ref[...]
        gate = jnp.dot(normed, gate_ref[e], preferred_element_type=f32)
        up = jnp.dot(normed, up_ref[e], preferred_element_type=f32)
        hidden.append((gate / (1.0 + jnp.exp(-gate)) * up * scale).astype(bf16))
    if loads:
        down_copy.wait()
    total = None
    for e, acts in enumerate(hidden):
        term = jnp.dot(acts, down_ref[e], preferred_element_type=f32)
        total = term if total is None else total + term
    keep_ref[...] = total[: rows // 2]
    send_ref[...] = total[rows // 2 :].astype(bf16)


def run_experts(mine, other, places, gain, gate, up, down, experts, n_sp, stream_shape, loads):
    rows = sum(array.shape[0] for array in mine)
    width = gain.shape[0]
    local = gate.shape[0]
    arrays = [*mine, *other, gain.reshape(1, width), gate, up, down]
    extra = [pltpu.VMEM(stream_shape, bf16)] if stream_shape else []
    if loads:
        extra.append(pltpu.VMEM(down.shape, bf16))
    return pl.pallas_call(
        functools.partial(
            experts_kernel, experts, lambda e, s: (e * n_sp + s) * local, places, stream_shape is not None, loads
        ),
        in_specs=[WHOLE] * (len(arrays) - 1) + [ANYWHERE if loads else WHOLE],
        out_specs=[WHOLE] * (2 + len(extra)),
        out_shape=[
            pltpu.VMEM((rows // 2, width), f32),
            pltpu.VMEM((rows // 2, width), bf16),
            *extra,
        ],
        scratch_shapes=[
            pltpu.VMEM((rows, width), bf16),
            pltpu.VMEM((rows, mine[0].shape[1] - width // 2), f32),
        ]
        + ([pltpu.SemaphoreType.DMA] if loads else []),
        compiler_params=pltpu.CompilerParams(vmem_limit_bytes=(12 if rows <= 256 else 48) * MIB),
        cost_estimate=pl.CostEstimate(
            flops=0, bytes_accessed=0, transcendentals=0
        ),
        name="experts",
    )(
        *[array if array.shape[0] == 1 else in_vmem(array) for array in arrays[:-1]],
        in_hbm(down) if loads else in_vmem(down),
    )


def place_rows(source_ref, target_ref, segments, first, columns, table_ref=None):
    half, rows = columns.size, target_ref.shape[0]
    for source, m, start, flip in segments:
        at = pl.multiple_of(start + (lax.axis_index("tp") ^ flip) * m, m)
        own, others = pl.ds(at, m), pl.ds(rows // 2 + at, m)
        upper, lower = slice(source, source + m), slice(source + m, source + 2 * m)
        for to, at in ((own, upper), (others, lower)) if first else ((own, lower), (others, upper)):
            target_ref[to, columns] = source_ref[at, :half]
            if table_ref is not None:
                table_ref[to, :] = source_ref[at, half:].astype(f32)


def start_kernel(segments, mine_ref, gain_ref, gate_ref, up_ref, partial_ref, rows_ref):
    half, hidden = rows_ref.shape[1], gate_ref.shape[2]
    place_rows(mine_ref, rows_ref, segments, True, pl.ds(0, half))
    at = pl.ds(pl.multiple_of(lax.axis_index("sp") * half, LANES), half)
    scaled = (rows_ref[...].astype(f32) * gain_ref[:, at]).astype(bf16)
    for e in range(gate_ref.shape[0]):
        for i, weight_ref in enumerate((gate_ref, up_ref)):
            to = slice((2 * e + i) * hidden, (2 * e + i + 1) * hidden)
            partial_ref[:, to] = jnp.dot(scaled, weight_ref[e, at, :], preferred_element_type=f32)


def finish_kernel(
    experts, first_of, segments, window, mine_ref, other_ref, partial_ref, gain_ref, gate_ref,
    up_ref, down_ref, keep_ref, send_ref, *refs
):
    *stream_ref, rows_ref, table_ref = refs
    rows, width = rows_ref.shape
    half, hidden = width // 2, gate_ref.shape[2]
    sp_index = lax.axis_index("sp")
    my_cols = pl.ds(pl.multiple_of(sp_index * half, LANES), half)
    other_cols = pl.ds(pl.multiple_of((1 - sp_index) * half, LANES), half)
    place_rows(mine_ref, rows_ref, segments, True, my_cols, table_ref)
    place_rows(other_ref, rows_ref, segments, False, other_cols)
    for out_ref in stream_ref:
        count, cut = out_ref.shape
        at = pl.ds(pl.multiple_of(lax.axis_index("tp") * cut, LANES), cut)
        out_ref[...] = rows_ref[:count, at]
    values = rows_ref[...].astype(f32)
    inverse = lax.rsqrt(jnp.mean(values * values, axis=1, keepdims=True) + norm_epsilon)
    scaled = (rows_ref[:, other_cols].astype(f32) * gain_ref[:, other_cols]).astype(bf16)
    first_expert = first_of(lax.axis_index("ep"), sp_index)
    table = table_ref[...]
    lane = lax.broadcasted_iota(jnp.int32, table.shape, 1)
    total = None
    for e in range(gate_ref.shape[0]):
        wanted = (lane == first_expert + e) | (lane == first_expert + e + experts)
        scale = jnp.sum(jnp.where(wanted, table, 0.0), axis=1, keepdims=True)
        sums = []
        for i, weight_ref in enumerate((gate_ref, up_ref)):
            at = slice((2 * e + i) * hidden, (2 * e + i + 1) * hidden)
            begun = jnp.concatenate(
                [
                    partial_ref[start + window : start + window + rows // 2, at]
                    for start in (0, partial_ref.shape[0] // 2)
                ],
                axis=0,
            )
            rest = jnp.dot(scaled, weight_ref[e, other_cols, :], preferred_element_type=f32)
            sums.append((begun + rest) * inverse)
        gate, up = sums
        acts = (gate / (1.0 + jnp.exp(-gate)) * up * scale).astype(bf16)
        term = jnp.dot(acts, down_ref[e], preferred_element_type=f32)
        total = term if total is None else total + term
    keep_ref[...] = total[: rows // 2]
    send_ref[...] = total[rows // 2 :].astype(bf16)


def start_experts(mine, segments, gain, gate, up):
    rows = mine.shape[0]
    return pl.pallas_call(
        functools.partial(start_kernel, segments),
        in_specs=[WHOLE] * 4,
        out_specs=WHOLE,
        out_shape=pltpu.VMEM((rows, 2 * gate.shape[0] * gate.shape[2]), f32),
        scratch_shapes=[pltpu.VMEM((rows, gain.shape[1] // 2), bf16)],
        compiler_params=pltpu.CompilerParams(vmem_limit_bytes=12 * MIB),
        cost_estimate=FREE,
        name="start_experts",
    )(in_vmem(mine), gain, in_vmem(gate), in_vmem(up))


def finish_experts(
    mine, other, partial, segments, window, count, gain, gate, up, down, experts, n_sp, stream_shape
):
    width, local = gain.shape[1], gate.shape[0]
    segments = tuple(
        (source, m, start - window, flip)
        for source, m, start, flip in segments
        if window <= start < window + count
    )
    return pl.pallas_call(
        functools.partial(
            finish_kernel, experts, lambda e, s: (e * n_sp + s) * local, segments, window
        ),
        in_specs=[WHOLE] * 7,
        out_specs=[WHOLE] * (3 if stream_shape else 2),
        out_shape=[
            pltpu.VMEM((count, width), f32),
            pltpu.VMEM((count, width), bf16),
            *([pltpu.VMEM(stream_shape, bf16)] if stream_shape else []),
        ],
        scratch_shapes=[
            pltpu.VMEM((2 * count, width), bf16),
            pltpu.VMEM((2 * count, mine.shape[1] - width // 2), f32),
        ],
        compiler_params=pltpu.CompilerParams(vmem_limit_bytes=12 * MIB),
        cost_estimate=FREE,
        name="finish_experts",
    )(in_vmem(mine), in_vmem(other), in_vmem(partial), gain, *map(in_vmem, (gate, up, down)))


def split_kernel(keep, back, keep_ref, send_ref):
    tp_index = lax.axis_index("tp")
    width = keep_ref.shape[1]
    mine = pl.ds(pl.multiple_of(tp_index * width, LANES), width)
    theirs = pl.ds(pl.multiple_of((1 - tp_index) * width, LANES), width)
    keep_ref[...] = keep[:, mine] + back[:, mine].astype(f32)
    send_ref[...] = (keep[:, theirs] + back[:, theirs].astype(f32)).astype(bf16)


def split(keep, back):
    shape = (keep.shape[0], keep.shape[1] // 2)
    return pl.pallas_call(
        split_kernel,
        in_specs=[WHOLE] * 2,
        out_specs=[WHOLE] * 2,
        out_shape=[pltpu.VMEM(shape, f32), pltpu.VMEM(shape, bf16)],
        compiler_params=pltpu.CompilerParams(vmem_limit_bytes=8 * MIB),
        cost_estimate=FREE,
        name="split",
    )(in_vmem(keep), in_vmem(back))


def part_kernel(keep, back, keep_ref, send_ref):
    rows = keep_ref.shape[0]
    keep_ref[...] = keep[:rows, :] + back[:rows, :].astype(f32)
    send_ref[...] = (keep[rows:, :] + back[rows:, :].astype(f32)).astype(bf16)


def part_near(keep, back):
    shape = (keep.shape[0] // 2, keep.shape[1])
    return pl.pallas_call(
        part_kernel,
        in_specs=[WHOLE] * 2,
        out_specs=[WHOLE] * 2,
        out_shape=[pltpu.VMEM(shape, f32), pltpu.VMEM(shape, bf16)],
        compiler_params=pltpu.CompilerParams(vmem_limit_bytes=8 * MIB),
        cost_estimate=FREE,
        name="part_near",
    )(in_vmem(keep), in_vmem(back))


def swap(array, axis, by=1):
    size = lax.axis_size(axis)
    return lax.ppermute(array, axis, [(i, i ^ by) for i in range(size)])


def shards(
    query,
    key_cache,
    value_cache,
    new_key,
    new_value,
    lengths,
    out_weight,
    residual,
    norm_gain,
    expert_ids,
    gate_weights,
    w_gate,
    w_up,
    w_down,
):
    rows = query.shape[0]
    width = residual.shape[1]
    n_ep, n_tp, n_sp = lax.axis_size("ep"), lax.axis_size("tp"), lax.axis_size("sp")
    tp_index = lax.axis_index("tp")
    experts = w_gate.shape[0] * n_ep * n_sp
    half = width // n_sp
    part = rows // n_tp
    out_width = width // n_tp
    heads_width = query.shape[1]

    packed, base, weight = attend(
        query, key_cache, value_cache, new_key, new_value, lengths, residual, expert_ids,
        gate_weights, out_weight, experts, n_sp
    )
    packed_other = swap(packed, "sp")
    stream_shape = (rows, out_width)
    if (n_ep, n_tp) == (4, 2) and part % 16 == 0:
        send_first, send_last, keep_first, keep_last, table_first, table_last = project(
            packed, packed_other, base, weight
        )
        first, last = swap(send_first, "tp"), swap(send_last, "tp")
        w_gate, _ = lax.optimization_barrier((w_gate, send_first))
        (w_gate,) = load(w_gate)
        first, w_gate = lax.optimization_barrier((first, w_gate))
        piece = jnp.concatenate([(keep_first + first.astype(f32)).astype(bf16), table_first], axis=1)
        second, third = swap(piece, "ep", 2), swap(piece, "ep", 3)
        piece_far = jnp.concatenate([(keep_last + last.astype(f32)).astype(bf16), table_last], axis=1)
        chip = jnp.concatenate([piece, piece_far], axis=0)
        next_chip = swap(chip, "ep", 1)
        w_up, _ = lax.optimization_barrier((w_up, chip))
        (w_up,) = load(w_up)
        second, third, w_up = lax.optimization_barrier((second, third, w_up))
        parts = jnp.concatenate([second, third], axis=0)
        far = swap(parts, "tp")
        w_down, _ = lax.optimization_barrier((w_down, parts))
        (w_down,) = load(w_down)
        far, next_chip, w_down = lax.optimization_barrier((far, next_chip, w_down))
        mine = jnp.concatenate([chip, next_chip, parts, far], axis=0)
        other = swap(mine, "sp")
        size = 2 * part
        segments = tuple(
            (i * size, part, k * rows, flip)
            for i, (k, flip) in enumerate(
                [(0, 0), (0, 1), (1, 0), (1, 1), (2, 0), (3, 0), (2, 1), (3, 1)]
            )
        )
        gain = norm_gain.reshape(1, width)
        partial = start_experts(mine, segments, gain, w_gate, w_up)
        keep, send = finish_experts(
            mine, other, partial, segments, 2 * rows, 2 * rows, gain, w_gate, w_up, w_down,
            experts, n_sp, None
        )
        partial, send = lax.optimization_barrier((partial, send))
        back = swap(send, "sp")
        keep_near, send_near, own_stream = finish_experts(
            mine, other, partial, segments, 0, 2 * rows, gain, w_gate, w_up, w_down,
            experts, n_sp, stream_shape
        )
        keep, send = split(keep, back)
        outer = keep + swap(send, "tp").astype(f32)
        second = swap(outer[:rows].astype(bf16), "ep", 2)
        third = swap(outer[rows:].astype(bf16), "ep", 3)
        keep_near, nearest = part_near(keep_near, swap(send_near, "sp"))
        keep_near, send_near = split(keep_near, swap(nearest, "ep", 1))
        final = own_stream.astype(f32) + second.astype(f32) + third.astype(f32)
        (final,) = lax.optimization_barrier((final,))
        return (final + keep_near + swap(send_near, "tp").astype(f32)).astype(bf16)

    def block_of(array, index):
        blocks = array.reshape(2, n_tp, part, -1)
        return lax.dynamic_slice_in_dim(blocks, index, 1, 1).reshape(2 * part, -1)

    def columns_of(array, index):
        return lax.dynamic_slice_in_dim(array, index * out_width, out_width, array.ndim - 1)

    both = jnp.concatenate([packed, packed_other], axis=0)
    terms = jnp.dot(both[:, :heads_width], weight, preferred_element_type=f32)
    residual_both = jnp.concatenate([base, packed_other[:, heads_width : heads_width + half]], axis=0)
    stream = block_of(terms, tp_index) + block_of(residual_both, tp_index).astype(f32)
    for by in range(1, n_tp):
        stream = stream + swap(block_of(terms, tp_index ^ by).astype(bf16), "tp", by).astype(f32)
    table = block_of(both[:, heads_width + half :], tp_index)
    piece = jnp.concatenate([stream.astype(bf16), table], axis=1)
    mine, places = [], []
    for by in range(n_ep):
        arrived = swap(piece, "ep", by) if by else piece
        for flip in range(n_tp):
            mine.append(swap(arrived, "tp", flip) if flip else arrived)
            places.append(((0, part, by * rows, flip),))
    if part % 16:
        gathered = jnp.stack(mine).reshape(n_ep, n_tp, 2, part, -1)
        bit = 1
        while bit < n_tp:
            flipped = gathered[:, jnp.array([j ^ bit for j in range(n_tp)])]
            gathered = jnp.where(tp_index & bit, flipped, gathered)
            bit *= 2
        mine = [gathered.transpose(2, 0, 1, 3, 4).reshape(2 * n_ep * rows, -1)]
        places = [((0, n_ep * rows, 0, None),)]
    other = [swap(array, "sp") for array in mine]
    keep, send, own_stream = run_experts(
        mine, other, tuple(places), norm_gain, w_gate, w_up, w_down, experts, n_sp, stream_shape, False
    )
    mixture = (keep + swap(send, "sp").astype(f32)).reshape(n_ep, rows, width)
    sums = columns_of(mixture, tp_index)
    for by in range(1, n_tp):
        sums = sums + swap(columns_of(mixture, tp_index ^ by).astype(bf16), "tp", by).astype(f32)
    final = sums[0]
    for by in range(1, n_ep):
        final = final + swap(sums[by].astype(bf16), "ep", by).astype(f32)
    return (final + own_stream.astype(f32)).astype(bf16)


def solution(mesh):
    placed = (
        P(("groups", "ep", "sp"), "tp"),
        P(("groups", "ep", "sp"), None, None),
        P(("groups", "ep", "sp"), None, None),
        P(("groups", "ep", "sp"), None),
        P(("groups", "ep", "sp"), None),
        P(("groups", "ep", "sp")),
        P("tp", "sp"),
        P(("groups", "ep", "sp"), None),
        P(),
        P(("groups", "ep", "sp"), None),
        P(("groups", "ep", "sp"), None),
        P(("ep", "sp"), None, "tp"),
        P(("ep", "sp"), None, "tp"),
        P(("ep", "sp"), "tp", None),
    )
    return jax.shard_map(
        shards,
        mesh=mesh,
        in_specs=placed,
        out_specs=P(("groups", "ep", "sp"), "tp"),
        check_vma=False,
    )
```

```python
import functools

import jax
import jax.numpy as jnp
from jax import lax
from jax.experimental import pallas as pl
from jax.experimental.pallas import tpu as pltpu
from jax.sharding import PartitionSpec as P

HEADS = 32
KV_HEADS = 4
HD = 128
LANES = 128
MIB = 2**20

masked_fill = -1e30
norm_epsilon = 1e-06
bf16 = jnp.bfloat16
f32 = jnp.float32


def attention_kernel(
    kv_count, per_group, chunk, experts, kv_block_of, lengths_hbm, query_hbm, key_hbm, value_hbm,
    new_key_hbm, new_value_hbm, residual_hbm, ids_hbm, gates_hbm, weight_hbm,
    packed_ref, base_ref, weight_ref,
    query_ref, key_ref, value_ref, new_key_ref, new_value_ref, residual_ref, ids_ref, gates_ref,
    rows_ref, lengths_ref, small_sems, cache_sems, weight_sem,
):
    rows, cached, kv_width = key_ref.shape
    heads = kv_count * per_group
    half = base_ref.shape[1]
    chunks = rows // chunk
    kv_at = pl.multiple_of(kv_block_of(lax.axis_index("tp")) * kv_width, HD)
    sp_index = lax.axis_index("sp")
    kv_cols = pl.ds(kv_at, kv_width)
    small = [
        pltpu.make_async_copy(source, target, small_sems.at[i])
        for i, (source, target) in enumerate(
            [
                (query_hbm, query_ref),
                (new_key_hbm.at[:, kv_cols], new_key_ref),
                (new_value_hbm.at[:, kv_cols], new_value_ref),
                (lengths_hbm, lengths_ref),
                (residual_hbm, residual_ref),
                (ids_hbm, ids_ref),
                (gates_hbm, gates_ref),
            ]
        )
    ]
    for copy in small[:4]:
        copy.start()
    cache_copies = []
    for i in range(chunks):
        at = pl.ds(i * chunk, chunk)
        pair = [
            pltpu.make_async_copy(
                source.at[at, :, kv_cols], target.at[at], cache_sems.at[which, i]
            )
            for which, (source, target) in enumerate(
                [(key_hbm, key_ref), (value_hbm, value_ref)]
            )
        ]
        for copy in pair:
            copy.start()
        cache_copies.append(pair)
    for copy in small[4:]:
        copy.start()
    weight_copy = pltpu.make_async_copy(weight_hbm, weight_ref, weight_sem)
    weight_copy.start()
    for copy in small[:4]:
        copy.wait()

    scaling = HD ** (-0.5)
    position = lax.broadcasted_iota(jnp.int32, (heads, cached), 1)
    for head in range(heads):
        kv, group = head // per_group, head % per_group
        rows_ref[kv, pl.ds(group, rows, stride=per_group), :] = query_ref[
            :, head * HD : (head + 1) * HD
        ].astype(f32)
    blank = jnp.zeros((per_group, HD), f32)
    for i in range(chunks):
        cache_copies[i][0].wait()
        scores, own = [], []
        for row in range(i * chunk, (i + 1) * chunk):
            at = slice(row * per_group, (row + 1) * per_group)
            queries = jnp.concatenate(
                [
                    jnp.concatenate(
                        [rows_ref[kv, at, :] if kv == other else blank for other in range(kv_count)],
                        axis=1,
                    )
                    for kv in range(kv_count)
                ],
                axis=0,
            )
            score = lax.dot_general(
                queries.astype(bf16),
                key_ref[row],
                (((1,), (1,)), ((), ())),
                preferred_element_type=f32,
            )
            visible = position < lengths_ref[row]
            scores.append(jnp.where(visible, score * scaling, masked_fill))
            fresh = new_key_ref[row : row + 1, :].astype(f32)
            own.append(jnp.sum(queries * fresh, axis=1, keepdims=True) * scaling)
        scores = jnp.concatenate(scores, axis=0)
        own = jnp.concatenate(own, axis=0)
        peak = jnp.maximum(jnp.max(scores, axis=1, keepdims=True), own)
        weights = jnp.exp(scores - peak)
        own_weight = jnp.exp(own - peak)
        inverse = 1.0 / (jnp.sum(weights, axis=1, keepdims=True) + own_weight)
        weights = weights.astype(bf16)
        cache_copies[i][1].wait()
        for row in range(i * chunk, (i + 1) * chunk):
            at = slice((row - i * chunk) * heads, (row - i * chunk + 1) * heads)
            blended = jnp.dot(weights[at], value_ref[row], preferred_element_type=f32)
            fresh = new_value_ref[row : row + 1, :].astype(f32)
            blended = (blended + own_weight[at] * fresh) * inverse[at]
            for kv in range(kv_count):
                rows_ref[kv, row * per_group : (row + 1) * per_group, :] = blended[
                    kv * per_group : (kv + 1) * per_group, kv * HD : (kv + 1) * HD
                ]
    for copy in small[4:]:
        copy.wait()
    width = heads * HD
    for head in range(heads):
        kv, group = head // per_group, head % per_group
        packed_ref[:, head * HD : (head + 1) * HD] = rows_ref[
            kv, pl.ds(group, rows, stride=per_group), :
        ].astype(bf16)
    packed_ref[:, width : width + half] = residual_ref[
        :, pl.ds(pl.multiple_of((1 - sp_index) * half, LANES), half)
    ]
    base_ref[...] = residual_ref[:, pl.ds(pl.multiple_of(sp_index * half, LANES), half)]
    spare = packed_ref.shape[1] - width - half
    place = lax.broadcasted_iota(jnp.int32, (spare, rows), 0)
    expert = jnp.where(place < experts, place, place - experts)
    table = jnp.zeros((spare, rows), f32)
    for k in range(ids_ref.shape[0]):
        table = table + jnp.where(ids_ref[k : k + 1, :] == expert, gates_ref[k : k + 1, :], 0.0)
    high = table.astype(bf16).astype(f32)
    table = jnp.where(place < experts, high, table - high)
    packed_ref[:, width + half :] = table.T.astype(bf16)
    weight_copy.wait()


def in_hbm(array):
    return pltpu.with_memory_space_constraint(array, pltpu.HBM)


def in_vmem(array):
    return pltpu.with_memory_space_constraint(array, pltpu.VMEM)


FREE = pl.CostEstimate(flops=0, bytes_accessed=0, transcendentals=0)
ANYWHERE = pl.BlockSpec(memory_space=pl.ANY)
WHOLE = pl.BlockSpec(memory_space=pltpu.VMEM)


def attend(
    query, key_cache, value_cache, new_key, new_value, lengths, residual, expert_ids,
    gate_weights, out_weight, experts, n_sp
):
    rows, width = query.shape
    cached = key_cache.shape[1]
    heads = width // HD
    grouping = HEADS // KV_HEADS
    kv_count = max(1, heads // grouping)
    per_group = heads // kv_count
    kv_width = kv_count * HD

    def kv_block_of(tp_index):
        return tp_index * heads // grouping // kv_count

    half = residual.shape[1] // n_sp
    spare = -(-2 * experts // LANES) * LANES
    chunk = min(16, rows)
    arrays = [
        lengths, query, key_cache, value_cache, new_key, new_value, residual, expert_ids.T,
        gate_weights.T, out_weight
    ]
    return pl.pallas_call(
        functools.partial(attention_kernel, kv_count, per_group, chunk, experts, kv_block_of),
        in_specs=[ANYWHERE] * len(arrays),
        out_specs=[WHOLE] * 3,
        out_shape=[
            pltpu.VMEM((rows, width + half + spare), bf16),
            pltpu.VMEM((rows, half), bf16),
            pltpu.VMEM(out_weight.shape, bf16),
        ],
        scratch_shapes=[
            pltpu.VMEM((rows, width), bf16),
            pltpu.VMEM((rows, cached, kv_width), bf16),
            pltpu.VMEM((rows, cached, kv_width), bf16),
            pltpu.VMEM((rows, kv_width), bf16),
            pltpu.VMEM((rows, kv_width), bf16),
            pltpu.VMEM(residual.shape, bf16),
            pltpu.VMEM((expert_ids.shape[1], rows), jnp.int32),
            pltpu.VMEM((expert_ids.shape[1], rows), f32),
            pltpu.VMEM((kv_count, rows * per_group, HD), f32),
            pltpu.SMEM((rows,), jnp.int32),
            pltpu.SemaphoreType.DMA((7,)),
            pltpu.SemaphoreType.DMA((2, rows // chunk)),
            pltpu.SemaphoreType.DMA,
        ],
        compiler_params=pltpu.CompilerParams(vmem_limit_bytes=24 * MIB),
        cost_estimate=FREE,
        name="attention",
    )(*map(in_hbm, arrays))


def project_kernel(
    packed_ref, other_ref, base_ref, weight_ref, send_first, send_last, keep_first, keep_last,
    table_first, table_last, terms_ref
):
    rows, half = base_ref.shape
    width = weight_ref.shape[0]
    part = rows // 2
    tp_index = lax.axis_index("tp")
    both = jnp.concatenate([packed_ref[:, :width], other_ref[:, :width]], axis=0)
    terms_ref[...] = jnp.dot(both, weight_ref[...], preferred_element_type=f32)
    for block, send_ref, keep_ref, table_ref in (
        (tp_index, send_last, keep_first, table_first),
        (1 - tp_index, send_first, keep_last, table_last),
    ):
        own = pl.ds(pl.multiple_of(block * part, part), part)
        for i, residual in enumerate((base_ref[own, :], other_ref[own, width : width + half])):
            to = slice(i * part, (i + 1) * part)
            terms = terms_ref[pl.ds(pl.multiple_of(i * rows + block * part, part), part), :]
            send_ref[to, :] = terms.astype(bf16)
            keep_ref[to, :] = terms + residual.astype(f32)
        table_ref[:part, :] = packed_ref[own, width + half :]
        table_ref[part:, :] = other_ref[own, width + half :]


def project(packed, packed_other, base, weight):
    shape = base.shape
    table = (shape[0], packed.shape[1] - weight.shape[0] - shape[1])
    return pl.pallas_call(
        project_kernel,
        in_specs=[WHOLE] * 4,
        out_specs=[WHOLE] * 6,
        out_shape=[
            *[pltpu.VMEM(shape, bf16)] * 2,
            *[pltpu.VMEM(shape, f32)] * 2,
            *[pltpu.VMEM(table, bf16)] * 2,
        ],
        scratch_shapes=[pltpu.VMEM((2 * shape[0], shape[1]), f32)],
        compiler_params=pltpu.CompilerParams(vmem_limit_bytes=8 * MIB),
        cost_estimate=FREE,
        name="project",
    )(*map(in_vmem, (packed, packed_other, base, weight)))


def load_kernel(*refs):
    *arrays, sems = refs
    count = len(arrays) // 2
    copies = [
        pltpu.make_async_copy(arrays[i], arrays[count + i], sems.at[i]) for i in range(count)
    ]
    for copy in copies:
        copy.start()
    for copy in copies:
        copy.wait()


def load(*arrays):
    return pl.pallas_call(
        load_kernel,
        in_specs=[ANYWHERE] * len(arrays),
        out_specs=[WHOLE] * len(arrays),
        out_shape=[pltpu.VMEM(array.shape, array.dtype) for array in arrays],
        scratch_shapes=[pltpu.SemaphoreType.DMA((len(arrays),))],
        compiler_params=pltpu.CompilerParams(vmem_limit_bytes=16 * MIB),
        cost_estimate=pl.CostEstimate(
            flops=0, bytes_accessed=0, transcendentals=0
        ),
        name="load_weights",
    )(*map(in_hbm, arrays))


def experts_kernel(experts, first_of, places, streams, loads, *refs):
    count = len(places)
    mine, other = refs[:count], refs[count : 2 * count]
    gain_ref, gate_ref, up_ref, down_ref, keep_ref, send_ref, *refs = refs[2 * count :]
    stream_ref = refs.pop(0) if streams else None
    if loads:
        down_hbm, down_ref, rows_ref, table_ref, sem = down_ref, *refs
        down_copy = pltpu.make_async_copy(down_hbm, down_ref, sem)
        down_copy.start()
    else:
        rows_ref, table_ref = refs
    half = rows_ref.shape[1] // 2
    rows = rows_ref.shape[0]
    sp_index = lax.axis_index("sp")
    tp_index = lax.axis_index("tp")
    my_cols = pl.ds(pl.multiple_of(sp_index * half, LANES), half)
    other_cols = pl.ds(pl.multiple_of((1 - sp_index) * half, LANES), half)
    for a, b, segments in zip(mine, other, places):
        for source, m, start, flip in segments:
            at = start if flip is None else pl.multiple_of(start + (tp_index ^ flip) * m, m)
            own, others = pl.ds(at, m), pl.ds(rows // 2 + at, m)
            upper, lower = slice(source, source + m), slice(source + m, source + 2 * m)
            rows_ref[own, my_cols] = a[upper, :half]
            rows_ref[others, my_cols] = a[lower, :half]
            rows_ref[own, other_cols] = b[lower, :half]
            rows_ref[others, other_cols] = b[upper, :half]
            table_ref[own, :] = a[upper, half:].astype(f32)
            table_ref[others, :] = a[lower, half:].astype(f32)
    if streams:
        count, width = stream_ref.shape
        out_cols = pl.ds(pl.multiple_of(tp_index * width, LANES), width)
        stream_ref[...] = rows_ref[:count, out_cols]
    values = rows_ref[...].astype(f32)
    inverse = lax.rsqrt(jnp.mean(values * values, axis=1, keepdims=True) + norm_epsilon)
    rows_ref[...] = (values * inverse * gain_ref[...]).astype(bf16)
    first_expert = first_of(lax.axis_index("ep"), sp_index)
    table = table_ref[...]
    lane = lax.broadcasted_iota(jnp.int32, table.shape, 1)
    hidden = []
    for e in range(gate_ref.shape[0]):
        wanted = (lane == first_expert + e) | (lane == first_expert + e + experts)
        scale = jnp.sum(jnp.where(wanted, table, 0.0), axis=1, keepdims=True)
        normed = rows_ref[...]
        gate = jnp.dot(normed, gate_ref[e], preferred_element_type=f32)
        up = jnp.dot(normed, up_ref[e], preferred_element_type=f32)
        hidden.append((gate / (1.0 + jnp.exp(-gate)) * up * scale).astype(bf16))
    if loads:
        down_copy.wait()
    total = None
    for e, acts in enumerate(hidden):
        term = jnp.dot(acts, down_ref[e], preferred_element_type=f32)
        total = term if total is None else total + term
    keep_ref[...] = total[: rows // 2]
    send_ref[...] = total[rows // 2 :].astype(bf16)


def run_experts(mine, other, places, gain, gate, up, down, experts, n_sp, stream_shape, loads):
    rows = sum(array.shape[0] for array in mine)
    width = gain.shape[0]
    local = gate.shape[0]
    arrays = [*mine, *other, gain.reshape(1, width), gate, up, down]
    extra = [pltpu.VMEM(stream_shape, bf16)] if stream_shape else []
    if loads:
        extra.append(pltpu.VMEM(down.shape, bf16))
    return pl.pallas_call(
        functools.partial(
            experts_kernel, experts, lambda e, s: (e * n_sp + s) * local, places, stream_shape is not None, loads
        ),
        in_specs=[WHOLE] * (len(arrays) - 1) + [ANYWHERE if loads else WHOLE],
        out_specs=[WHOLE] * (2 + len(extra)),
        out_shape=[
            pltpu.VMEM((rows // 2, width), f32),
            pltpu.VMEM((rows // 2, width), bf16),
            *extra,
        ],
        scratch_shapes=[
            pltpu.VMEM((rows, width), bf16),
            pltpu.VMEM((rows, mine[0].shape[1] - width // 2), f32),
        ]
        + ([pltpu.SemaphoreType.DMA] if loads else []),
        compiler_params=pltpu.CompilerParams(vmem_limit_bytes=(12 if rows <= 256 else 48) * MIB),
        cost_estimate=pl.CostEstimate(
            flops=0, bytes_accessed=0, transcendentals=0
        ),
        name="experts",
    )(
        *[array if array.shape[0] == 1 else in_vmem(array) for array in arrays[:-1]],
        in_hbm(down) if loads else in_vmem(down),
    )


def place_rows(source_ref, target_ref, segments, first, columns, table_ref=None):
    half, rows = columns.size, target_ref.shape[0]
    for source, m, start, flip in segments:
        at = pl.multiple_of(start + (lax.axis_index("tp") ^ flip) * m, m)
        own, others = pl.ds(at, m), pl.ds(rows // 2 + at, m)
        upper, lower = slice(source, source + m), slice(source + m, source + 2 * m)
        for to, at in ((own, upper), (others, lower)) if first else ((own, lower), (others, upper)):
            target_ref[to, columns] = source_ref[at, :half]
            if table_ref is not None:
                table_ref[to, :] = source_ref[at, half:].astype(f32)


def start_kernel(segments, mine_ref, gain_ref, gate_ref, up_ref, partial_ref, rows_ref):
    half, hidden = rows_ref.shape[1], gate_ref.shape[2]
    place_rows(mine_ref, rows_ref, segments, True, pl.ds(0, half))
    at = pl.ds(pl.multiple_of(lax.axis_index("sp") * half, LANES), half)
    scaled = (rows_ref[...].astype(f32) * gain_ref[:, at]).astype(bf16)
    for e in range(gate_ref.shape[0]):
        for i, weight_ref in enumerate((gate_ref, up_ref)):
            to = slice((2 * e + i) * hidden, (2 * e + i + 1) * hidden)
            partial_ref[:, to] = jnp.dot(scaled, weight_ref[e, at, :], preferred_element_type=f32)


def finish_kernel(
    experts, first_of, segments, window, mine_ref, other_ref, partial_ref, gain_ref, gate_ref,
    up_ref, down_ref, keep_ref, send_ref, *refs
):
    *stream_ref, rows_ref, table_ref = refs
    rows, width = rows_ref.shape
    half, hidden = width // 2, gate_ref.shape[2]
    sp_index = lax.axis_index("sp")
    my_cols = pl.ds(pl.multiple_of(sp_index * half, LANES), half)
    other_cols = pl.ds(pl.multiple_of((1 - sp_index) * half, LANES), half)
    place_rows(mine_ref, rows_ref, segments, True, my_cols, table_ref)
    place_rows(other_ref, rows_ref, segments, False, other_cols)
    for out_ref in stream_ref:
        count, cut = out_ref.shape
        at = pl.ds(pl.multiple_of(lax.axis_index("tp") * cut, LANES), cut)
        out_ref[...] = rows_ref[:count, at]
    values = rows_ref[...].astype(f32)
    inverse = lax.rsqrt(jnp.mean(values * values, axis=1, keepdims=True) + norm_epsilon)
    scaled = (rows_ref[:, other_cols].astype(f32) * gain_ref[:, other_cols]).astype(bf16)
    first_expert = first_of(lax.axis_index("ep"), sp_index)
    table = table_ref[...]
    lane = lax.broadcasted_iota(jnp.int32, table.shape, 1)
    total = None
    for e in range(gate_ref.shape[0]):
        wanted = (lane == first_expert + e) | (lane == first_expert + e + experts)
        scale = jnp.sum(jnp.where(wanted, table, 0.0), axis=1, keepdims=True)
        sums = []
        for i, weight_ref in enumerate((gate_ref, up_ref)):
            at = slice((2 * e + i) * hidden, (2 * e + i + 1) * hidden)
            begun = jnp.concatenate(
                [
                    partial_ref[start + window : start + window + rows // 2, at]
                    for start in (0, partial_ref.shape[0] // 2)
                ],
                axis=0,
            )
            rest = jnp.dot(scaled, weight_ref[e, other_cols, :], preferred_element_type=f32)
            sums.append((begun + rest) * inverse)
        gate, up = sums
        acts = (gate / (1.0 + jnp.exp(-gate)) * up * scale).astype(bf16)
        term = jnp.dot(acts, down_ref[e], preferred_element_type=f32)
        total = term if total is None else total + term
    keep_ref[...] = total[: rows // 2]
    send_ref[...] = total[rows // 2 :].astype(bf16)


def start_experts(mine, segments, gain, gate, up):
    rows = mine.shape[0]
    return pl.pallas_call(
        functools.partial(start_kernel, segments),
        in_specs=[WHOLE] * 4,
        out_specs=WHOLE,
        out_shape=pltpu.VMEM((rows, 2 * gate.shape[0] * gate.shape[2]), f32),
        scratch_shapes=[pltpu.VMEM((rows, gain.shape[1] // 2), bf16)],
        compiler_params=pltpu.CompilerParams(vmem_limit_bytes=12 * MIB),
        cost_estimate=FREE,
        name="start_experts",
    )(in_vmem(mine), gain, in_vmem(gate), in_vmem(up))


def finish_experts(
    mine, other, partial, segments, window, count, gain, gate, up, down, experts, n_sp, stream_shape
):
    width, local = gain.shape[1], gate.shape[0]
    segments = tuple(
        (source, m, start - window, flip)
        for source, m, start, flip in segments
        if window <= start < window + count
    )
    return pl.pallas_call(
        functools.partial(
            finish_kernel, experts, lambda e, s: (e * n_sp + s) * local, segments, window
        ),
        in_specs=[WHOLE] * 7,
        out_specs=[WHOLE] * (3 if stream_shape else 2),
        out_shape=[
            pltpu.VMEM((count, width), f32),
            pltpu.VMEM((count, width), bf16),
            *([pltpu.VMEM(stream_shape, bf16)] if stream_shape else []),
        ],
        scratch_shapes=[
            pltpu.VMEM((2 * count, width), bf16),
            pltpu.VMEM((2 * count, mine.shape[1] - width // 2), f32),
        ],
        compiler_params=pltpu.CompilerParams(vmem_limit_bytes=12 * MIB),
        cost_estimate=FREE,
        name="finish_experts",
    )(in_vmem(mine), in_vmem(other), in_vmem(partial), gain, *map(in_vmem, (gate, up, down)))


def split_kernel(keep, back, *out_refs):
    count = len(out_refs) // 2
    tp_index = lax.axis_index("tp")
    rows, width = out_refs[0].shape
    mine = pl.ds(pl.multiple_of(tp_index * width, LANES), width)
    theirs = pl.ds(pl.multiple_of((1 - tp_index) * width, LANES), width)
    for i, (keep_ref, send_ref) in enumerate(zip(out_refs[:count], out_refs[count:])):
        at = slice(i * rows, (i + 1) * rows)
        keep_ref[...] = keep[at, mine] + back[at, mine].astype(f32)
        send_ref[...] = (keep[at, theirs] + back[at, theirs].astype(f32)).astype(bf16)


def split(pieces, keep, back):
    shape = (keep.shape[0] // pieces, keep.shape[1] // 2)
    return pl.pallas_call(
        split_kernel,
        in_specs=[WHOLE] * 2,
        out_specs=[WHOLE] * (2 * pieces),
        out_shape=[pltpu.VMEM(shape, f32)] * pieces + [pltpu.VMEM(shape, bf16)] * pieces,
        compiler_params=pltpu.CompilerParams(vmem_limit_bytes=8 * MIB),
        cost_estimate=FREE,
        name="split",
    )(in_vmem(keep), in_vmem(back))


def part_kernel(keep, back, keep_ref, send_ref):
    rows = keep_ref.shape[0]
    keep_ref[...] = keep[:rows, :] + back[:rows, :].astype(f32)
    send_ref[...] = (keep[rows:, :] + back[rows:, :].astype(f32)).astype(bf16)


def part_near(keep, back):
    shape = (keep.shape[0] // 2, keep.shape[1])
    return pl.pallas_call(
        part_kernel,
        in_specs=[WHOLE] * 2,
        out_specs=[WHOLE] * 2,
        out_shape=[pltpu.VMEM(shape, f32), pltpu.VMEM(shape, bf16)],
        compiler_params=pltpu.CompilerParams(vmem_limit_bytes=8 * MIB),
        cost_estimate=FREE,
        name="part_near",
    )(in_vmem(keep), in_vmem(back))


def swap(array, axis, by=1):
    size = lax.axis_size(axis)
    return lax.ppermute(array, axis, [(i, i ^ by) for i in range(size)])


def shards(
    query,
    key_cache,
    value_cache,
    new_key,
    new_value,
    lengths,
    out_weight,
    residual,
    norm_gain,
    expert_ids,
    gate_weights,
    w_gate,
    w_up,
    w_down,
):
    rows = query.shape[0]
    width = residual.shape[1]
    n_ep, n_tp, n_sp = lax.axis_size("ep"), lax.axis_size("tp"), lax.axis_size("sp")
    tp_index = lax.axis_index("tp")
    experts = w_gate.shape[0] * n_ep * n_sp
    half = width // n_sp
    part = rows // n_tp
    out_width = width // n_tp
    heads_width = query.shape[1]

    packed, base, weight = attend(
        query, key_cache, value_cache, new_key, new_value, lengths, residual, expert_ids,
        gate_weights, out_weight, experts, n_sp
    )
    packed_other = swap(packed, "sp")
    stream_shape = (rows, out_width)
    if (n_ep, n_tp) == (4, 2) and part % 16 == 0:
        send_first, send_last, keep_first, keep_last, table_first, table_last = project(
            packed, packed_other, base, weight
        )
        first, last = swap(send_first, "tp"), swap(send_last, "tp")
        w_gate, _ = lax.optimization_barrier((w_gate, send_first))
        (w_gate,) = load(w_gate)
        first, w_gate = lax.optimization_barrier((first, w_gate))
        piece = jnp.concatenate([(keep_first + first.astype(f32)).astype(bf16), table_first], axis=1)
        second, third = swap(piece, "ep", 2), swap(piece, "ep", 3)
        piece_far = jnp.concatenate([(keep_last + last.astype(f32)).astype(bf16), table_last], axis=1)
        chip = jnp.concatenate([piece, piece_far], axis=0)
        next_chip = swap(chip, "ep", 1)
        w_up, _ = lax.optimization_barrier((w_up, chip))
        (w_up,) = load(w_up)
        second, w_up = lax.optimization_barrier((second, w_up))
        second_far, third_far = swap(second, "tp"), swap(third, "tp")
        w_down, _, _ = lax.optimization_barrier((w_down, second, third))
        (w_down,) = load(w_down)
        second_far, third_far, next_chip, w_down = lax.optimization_barrier(
            (second_far, third_far, next_chip, w_down)
        )
        mine = jnp.concatenate(
            [chip, next_chip, second, third, second_far, third_far], axis=0
        )
        other = swap(mine, "sp")
        size = 2 * part
        segments = tuple(
            (i * size, part, k * rows, flip)
            for i, (k, flip) in enumerate(
                [(0, 0), (0, 1), (1, 0), (1, 1), (2, 0), (3, 0), (2, 1), (3, 1)]
            )
        )
        gain = norm_gain.reshape(1, width)
        partial = start_experts(mine, segments, gain, w_gate, w_up)
        keep, send = finish_experts(
            mine, other, partial, segments, 2 * rows, 2 * rows, gain, w_gate, w_up, w_down,
            experts, n_sp, None
        )
        partial, send = lax.optimization_barrier((partial, send))
        back = swap(send, "sp")
        keep_near, send_near, own_stream = finish_experts(
            mine, other, partial, segments, 0, 2 * rows, gain, w_gate, w_up, w_down,
            experts, n_sp, stream_shape
        )
        keep_second, keep_third, send_second, send_third = split(2, keep, back)
        second = keep_second + swap(send_second, "tp").astype(f32)
        third = keep_third + swap(send_third, "tp").astype(f32)
        second, third = swap(second.astype(bf16), "ep", 2), swap(third.astype(bf16), "ep", 3)
        keep_near, nearest = part_near(keep_near, swap(send_near, "sp"))
        keep_near, send_near = split(1, keep_near, swap(nearest, "ep", 1))
        final = own_stream.astype(f32) + second.astype(f32) + third.astype(f32)
        (final,) = lax.optimization_barrier((final,))
        return (final + keep_near + swap(send_near, "tp").astype(f32)).astype(bf16)

    def block_of(array, index):
        blocks = array.reshape(2, n_tp, part, -1)
        return lax.dynamic_slice_in_dim(blocks, index, 1, 1).reshape(2 * part, -1)

    def columns_of(array, index):
        return lax.dynamic_slice_in_dim(array, index * out_width, out_width, array.ndim - 1)

    both = jnp.concatenate([packed, packed_other], axis=0)
    terms = jnp.dot(both[:, :heads_width], weight, preferred_element_type=f32)
    residual_both = jnp.concatenate([base, packed_other[:, heads_width : heads_width + half]], axis=0)
    stream = block_of(terms, tp_index) + block_of(residual_both, tp_index).astype(f32)
    for by in range(1, n_tp):
        stream = stream + swap(block_of(terms, tp_index ^ by).astype(bf16), "tp", by).astype(f32)
    table = block_of(both[:, heads_width + half :], tp_index)
    piece = jnp.concatenate([stream.astype(bf16), table], axis=1)
    mine, places = [], []
    for by in range(n_ep):
        arrived = swap(piece, "ep", by) if by else piece
        for flip in range(n_tp):
            mine.append(swap(arrived, "tp", flip) if flip else arrived)
            places.append(((0, part, by * rows, flip),))
    if part % 16:
        gathered = jnp.stack(mine).reshape(n_ep, n_tp, 2, part, -1)
        bit = 1
        while bit < n_tp:
            flipped = gathered[:, jnp.array([j ^ bit for j in range(n_tp)])]
            gathered = jnp.where(tp_index & bit, flipped, gathered)
            bit *= 2
        mine = [gathered.transpose(2, 0, 1, 3, 4).reshape(2 * n_ep * rows, -1)]
        places = [((0, n_ep * rows, 0, None),)]
    other = [swap(array, "sp") for array in mine]
    keep, send, own_stream = run_experts(
        mine, other, tuple(places), norm_gain, w_gate, w_up, w_down, experts, n_sp, stream_shape, False
    )
    mixture = (keep + swap(send, "sp").astype(f32)).reshape(n_ep, rows, width)
    sums = columns_of(mixture, tp_index)
    for by in range(1, n_tp):
        sums = sums + swap(columns_of(mixture, tp_index ^ by).astype(bf16), "tp", by).astype(f32)
    final = sums[0]
    for by in range(1, n_ep):
        final = final + swap(sums[by].astype(bf16), "ep", by).astype(f32)
    return (final + own_stream.astype(f32)).astype(bf16)


def solution(mesh):
    placed = (
        P(("groups", "ep", "sp"), "tp"),
        P(("groups", "ep", "sp"), None, None),
        P(("groups", "ep", "sp"), None, None),
        P(("groups", "ep", "sp"), None),
        P(("groups", "ep", "sp"), None),
        P(("groups", "ep", "sp")),
        P("tp", "sp"),
        P(("groups", "ep", "sp"), None),
        P(),
        P(("groups", "ep", "sp"), None),
        P(("groups", "ep", "sp"), None),
        P(("ep", "sp"), None, "tp"),
        P(("ep", "sp"), None, "tp"),
        P(("ep", "sp"), "tp", None),
    )
    return jax.shard_map(
        shards,
        mesh=mesh,
        in_specs=placed,
        out_specs=P(("groups", "ep", "sp"), "tp"),
        check_vma=False,
    )
```

```python
import functools

import jax
import jax.numpy as jnp
from jax import lax
from jax.experimental import pallas as pl
from jax.experimental.pallas import tpu as pltpu
from jax.sharding import PartitionSpec as P

HEADS = 32
KV_HEADS = 4
HD = 128
LANES = 128
MIB = 2**20

masked_fill = -1e30
norm_epsilon = 1e-06
bf16 = jnp.bfloat16
f32 = jnp.float32


def attention_kernel(
    kv_count, per_group, chunk, experts, kv_block_of, lengths_hbm, query_hbm, key_hbm, value_hbm,
    new_key_hbm, new_value_hbm, residual_hbm, ids_hbm, gates_hbm, weight_hbm,
    packed_ref, base_ref, weight_ref,
    query_ref, key_ref, value_ref, new_key_ref, new_value_ref, residual_ref, ids_ref, gates_ref,
    rows_ref, lengths_ref, small_sems, cache_sems, weight_sem,
):
    rows, cached, kv_width = key_ref.shape
    heads = kv_count * per_group
    half = base_ref.shape[1]
    chunks = rows // chunk
    kv_at = pl.multiple_of(kv_block_of(lax.axis_index("tp")) * kv_width, HD)
    sp_index = lax.axis_index("sp")
    kv_cols = pl.ds(kv_at, kv_width)
    small = [
        pltpu.make_async_copy(source, target, small_sems.at[i])
        for i, (source, target) in enumerate(
            [
                (query_hbm, query_ref),
                (new_key_hbm.at[:, kv_cols], new_key_ref),
                (new_value_hbm.at[:, kv_cols], new_value_ref),
                (lengths_hbm, lengths_ref),
                (residual_hbm, residual_ref),
                (ids_hbm, ids_ref),
                (gates_hbm, gates_ref),
            ]
        )
    ]
    for copy in small[:4]:
        copy.start()
    cache_copies = []
    for i in range(chunks):
        at = pl.ds(i * chunk, chunk)
        pair = [
            pltpu.make_async_copy(
                source.at[at, :, kv_cols], target.at[at], cache_sems.at[which, i]
            )
            for which, (source, target) in enumerate(
                [(key_hbm, key_ref), (value_hbm, value_ref)]
            )
        ]
        for copy in pair:
            copy.start()
        cache_copies.append(pair)
    for copy in small[4:]:
        copy.start()
    weight_copy = pltpu.make_async_copy(weight_hbm, weight_ref, weight_sem)
    weight_copy.start()
    for copy in small[:4]:
        copy.wait()

    scaling = HD ** (-0.5)
    position = lax.broadcasted_iota(jnp.int32, (heads, cached), 1)
    for head in range(heads):
        kv, group = head // per_group, head % per_group
        rows_ref[kv, pl.ds(group, rows, stride=per_group), :] = query_ref[
            :, head * HD : (head + 1) * HD
        ].astype(f32)
    blank = jnp.zeros((per_group, HD), f32)
    for i in range(chunks):
        cache_copies[i][0].wait()
        scores, own = [], []
        for row in range(i * chunk, (i + 1) * chunk):
            at = slice(row * per_group, (row + 1) * per_group)
            queries = jnp.concatenate(
                [
                    jnp.concatenate(
                        [rows_ref[kv, at, :] if kv == other else blank for other in range(kv_count)],
                        axis=1,
                    )
                    for kv in range(kv_count)
                ],
                axis=0,
            )
            score = lax.dot_general(
                queries.astype(bf16),
                key_ref[row],
                (((1,), (1,)), ((), ())),
                preferred_element_type=f32,
            )
            visible = position < lengths_ref[row]
            scores.append(jnp.where(visible, score * scaling, masked_fill))
            fresh = new_key_ref[row : row + 1, :].astype(f32)
            own.append(jnp.sum(queries * fresh, axis=1, keepdims=True) * scaling)
        scores = jnp.concatenate(scores, axis=0)
        own = jnp.concatenate(own, axis=0)
        peak = jnp.maximum(jnp.max(scores, axis=1, keepdims=True), own)
        weights = jnp.exp(scores - peak)
        own_weight = jnp.exp(own - peak)
        inverse = 1.0 / (jnp.sum(weights, axis=1, keepdims=True) + own_weight)
        weights = weights.astype(bf16)
        cache_copies[i][1].wait()
        for row in range(i * chunk, (i + 1) * chunk):
            at = slice((row - i * chunk) * heads, (row - i * chunk + 1) * heads)
            blended = jnp.dot(weights[at], value_ref[row], preferred_element_type=f32)
            fresh = new_value_ref[row : row + 1, :].astype(f32)
            blended = (blended + own_weight[at] * fresh) * inverse[at]
            for kv in range(kv_count):
                rows_ref[kv, row * per_group : (row + 1) * per_group, :] = blended[
                    kv * per_group : (kv + 1) * per_group, kv * HD : (kv + 1) * HD
                ]
    for copy in small[4:]:
        copy.wait()
    width = heads * HD
    for head in range(heads):
        kv, group = head // per_group, head % per_group
        packed_ref[:, head * HD : (head + 1) * HD] = rows_ref[
            kv, pl.ds(group, rows, stride=per_group), :
        ].astype(bf16)
    packed_ref[:, width : width + half] = residual_ref[
        :, pl.ds(pl.multiple_of((1 - sp_index) * half, LANES), half)
    ]
    base_ref[...] = residual_ref[:, pl.ds(pl.multiple_of(sp_index * half, LANES), half)]
    spare = packed_ref.shape[1] - width - half
    place = lax.broadcasted_iota(jnp.int32, (spare, rows), 0)
    expert = jnp.where(place < experts, place, place - experts)
    table = jnp.zeros((spare, rows), f32)
    for k in range(ids_ref.shape[0]):
        table = table + jnp.where(ids_ref[k : k + 1, :] == expert, gates_ref[k : k + 1, :], 0.0)
    high = table.astype(bf16).astype(f32)
    table = jnp.where(place < experts, high, table - high)
    packed_ref[:, width + half :] = table.T.astype(bf16)
    weight_copy.wait()


def in_hbm(array):
    return pltpu.with_memory_space_constraint(array, pltpu.HBM)


def in_vmem(array):
    return pltpu.with_memory_space_constraint(array, pltpu.VMEM)


FREE = pl.CostEstimate(flops=0, bytes_accessed=0, transcendentals=0)
ANYWHERE = pl.BlockSpec(memory_space=pl.ANY)
WHOLE = pl.BlockSpec(memory_space=pltpu.VMEM)


def attend(
    query, key_cache, value_cache, new_key, new_value, lengths, residual, expert_ids,
    gate_weights, out_weight, experts, n_sp
):
    rows, width = query.shape
    cached = key_cache.shape[1]
    heads = width // HD
    grouping = HEADS // KV_HEADS
    kv_count = max(1, heads // grouping)
    per_group = heads // kv_count
    kv_width = kv_count * HD

    def kv_block_of(tp_index):
        return tp_index * heads // grouping // kv_count

    half = residual.shape[1] // n_sp
    spare = -(-2 * experts // LANES) * LANES
    chunk = min(16, rows)
    arrays = [
        lengths, query, key_cache, value_cache, new_key, new_value, residual, expert_ids.T,
        gate_weights.T, out_weight
    ]
    return pl.pallas_call(
        functools.partial(attention_kernel, kv_count, per_group, chunk, experts, kv_block_of),
        in_specs=[ANYWHERE] * len(arrays),
        out_specs=[WHOLE] * 3,
        out_shape=[
            pltpu.VMEM((rows, width + half + spare), bf16),
            pltpu.VMEM((rows, half), bf16),
            pltpu.VMEM(out_weight.shape, bf16),
        ],
        scratch_shapes=[
            pltpu.VMEM((rows, width), bf16),
            pltpu.VMEM((rows, cached, kv_width), bf16),
            pltpu.VMEM((rows, cached, kv_width), bf16),
            pltpu.VMEM((rows, kv_width), bf16),
            pltpu.VMEM((rows, kv_width), bf16),
            pltpu.VMEM(residual.shape, bf16),
            pltpu.VMEM((expert_ids.shape[1], rows), jnp.int32),
            pltpu.VMEM((expert_ids.shape[1], rows), f32),
            pltpu.VMEM((kv_count, rows * per_group, HD), f32),
            pltpu.SMEM((rows,), jnp.int32),
            pltpu.SemaphoreType.DMA((7,)),
            pltpu.SemaphoreType.DMA((2, rows // chunk)),
            pltpu.SemaphoreType.DMA,
        ],
        compiler_params=pltpu.CompilerParams(vmem_limit_bytes=24 * MIB),
        cost_estimate=FREE,
        name="attention",
    )(*map(in_hbm, arrays))


def project_kernel(
    packed_ref, other_ref, base_ref, weight_ref, send_first, send_last, keep_first, keep_last,
    table_first, table_last, terms_ref
):
    rows, half = base_ref.shape
    width = weight_ref.shape[0]
    part = rows // 2
    tp_index = lax.axis_index("tp")
    both = jnp.concatenate([packed_ref[:, :width], other_ref[:, :width]], axis=0)
    terms_ref[...] = jnp.dot(both, weight_ref[...], preferred_element_type=f32)
    for block, send_ref, keep_ref, table_ref in (
        (tp_index, send_last, keep_first, table_first),
        (1 - tp_index, send_first, keep_last, table_last),
    ):
        own = pl.ds(pl.multiple_of(block * part, part), part)
        for i, residual in enumerate((base_ref[own, :], other_ref[own, width : width + half])):
            to = slice(i * part, (i + 1) * part)
            terms = terms_ref[pl.ds(pl.multiple_of(i * rows + block * part, part), part), :]
            send_ref[to, :] = terms.astype(bf16)
            keep_ref[to, :] = terms + residual.astype(f32)
        table_ref[:part, :] = packed_ref[own, width + half :]
        table_ref[part:, :] = other_ref[own, width + half :]


def project(packed, packed_other, base, weight):
    shape = base.shape
    table = (shape[0], packed.shape[1] - weight.shape[0] - shape[1])
    return pl.pallas_call(
        project_kernel,
        in_specs=[WHOLE] * 4,
        out_specs=[WHOLE] * 6,
        out_shape=[
            *[pltpu.VMEM(shape, bf16)] * 2,
            *[pltpu.VMEM(shape, f32)] * 2,
            *[pltpu.VMEM(table, bf16)] * 2,
        ],
        scratch_shapes=[pltpu.VMEM((2 * shape[0], shape[1]), f32)],
        compiler_params=pltpu.CompilerParams(vmem_limit_bytes=8 * MIB),
        cost_estimate=FREE,
        name="project",
    )(*map(in_vmem, (packed, packed_other, base, weight)))


def load_kernel(*refs):
    *arrays, sems = refs
    count = len(arrays) // 2
    copies = [
        pltpu.make_async_copy(arrays[i], arrays[count + i], sems.at[i]) for i in range(count)
    ]
    for copy in copies:
        copy.start()
    for copy in copies:
        copy.wait()


def load(*arrays):
    return pl.pallas_call(
        load_kernel,
        in_specs=[ANYWHERE] * len(arrays),
        out_specs=[WHOLE] * len(arrays),
        out_shape=[pltpu.VMEM(array.shape, array.dtype) for array in arrays],
        scratch_shapes=[pltpu.SemaphoreType.DMA((len(arrays),))],
        compiler_params=pltpu.CompilerParams(vmem_limit_bytes=16 * MIB),
        cost_estimate=pl.CostEstimate(
            flops=0, bytes_accessed=0, transcendentals=0
        ),
        name="load_weights",
    )(*map(in_hbm, arrays))


def experts_kernel(experts, first_of, places, streams, loads, *refs):
    count = len(places)
    mine, other = refs[:count], refs[count : 2 * count]
    gain_ref, gate_ref, up_ref, down_ref, keep_ref, send_ref, *refs = refs[2 * count :]
    stream_ref = refs.pop(0) if streams else None
    if loads:
        down_hbm, down_ref, rows_ref, table_ref, sem = down_ref, *refs
        down_copy = pltpu.make_async_copy(down_hbm, down_ref, sem)
        down_copy.start()
    else:
        rows_ref, table_ref = refs
    half = rows_ref.shape[1] // 2
    rows = rows_ref.shape[0]
    sp_index = lax.axis_index("sp")
    tp_index = lax.axis_index("tp")
    my_cols = pl.ds(pl.multiple_of(sp_index * half, LANES), half)
    other_cols = pl.ds(pl.multiple_of((1 - sp_index) * half, LANES), half)
    for a, b, segments in zip(mine, other, places):
        for source, m, start, flip in segments:
            at = start if flip is None else pl.multiple_of(start + (tp_index ^ flip) * m, m)
            own, others = pl.ds(at, m), pl.ds(rows // 2 + at, m)
            upper, lower = slice(source, source + m), slice(source + m, source + 2 * m)
            rows_ref[own, my_cols] = a[upper, :half]
            rows_ref[others, my_cols] = a[lower, :half]
            rows_ref[own, other_cols] = b[lower, :half]
            rows_ref[others, other_cols] = b[upper, :half]
            table_ref[own, :] = a[upper, half:].astype(f32)
            table_ref[others, :] = a[lower, half:].astype(f32)
    if streams:
        count, width = stream_ref.shape
        out_cols = pl.ds(pl.multiple_of(tp_index * width, LANES), width)
        stream_ref[...] = rows_ref[:count, out_cols]
    values = rows_ref[...].astype(f32)
    inverse = lax.rsqrt(jnp.mean(values * values, axis=1, keepdims=True) + norm_epsilon)
    rows_ref[...] = (values * inverse * gain_ref[...]).astype(bf16)
    first_expert = first_of(lax.axis_index("ep"), sp_index)
    table = table_ref[...]
    lane = lax.broadcasted_iota(jnp.int32, table.shape, 1)
    hidden = []
    for e in range(gate_ref.shape[0]):
        wanted = (lane == first_expert + e) | (lane == first_expert + e + experts)
        scale = jnp.sum(jnp.where(wanted, table, 0.0), axis=1, keepdims=True)
        normed = rows_ref[...]
        gate = jnp.dot(normed, gate_ref[e], preferred_element_type=f32)
        up = jnp.dot(normed, up_ref[e], preferred_element_type=f32)
        hidden.append((gate / (1.0 + jnp.exp(-gate)) * up * scale).astype(bf16))
    if loads:
        down_copy.wait()
    total = None
    for e, acts in enumerate(hidden):
        term = jnp.dot(acts, down_ref[e], preferred_element_type=f32)
        total = term if total is None else total + term
    keep_ref[...] = total[: rows // 2]
    send_ref[...] = total[rows // 2 :].astype(bf16)


def run_experts(mine, other, places, gain, gate, up, down, experts, n_sp, stream_shape, loads):
    rows = sum(array.shape[0] for array in mine)
    width = gain.shape[0]
    local = gate.shape[0]
    arrays = [*mine, *other, gain.reshape(1, width), gate, up, down]
    extra = [pltpu.VMEM(stream_shape, bf16)] if stream_shape else []
    if loads:
        extra.append(pltpu.VMEM(down.shape, bf16))
    return pl.pallas_call(
        functools.partial(
            experts_kernel, experts, lambda e, s: (e * n_sp + s) * local, places, stream_shape is not None, loads
        ),
        in_specs=[WHOLE] * (len(arrays) - 1) + [ANYWHERE if loads else WHOLE],
        out_specs=[WHOLE] * (2 + len(extra)),
        out_shape=[
            pltpu.VMEM((rows // 2, width), f32),
            pltpu.VMEM((rows // 2, width), bf16),
            *extra,
        ],
        scratch_shapes=[
            pltpu.VMEM((rows, width), bf16),
            pltpu.VMEM((rows, mine[0].shape[1] - width // 2), f32),
        ]
        + ([pltpu.SemaphoreType.DMA] if loads else []),
        compiler_params=pltpu.CompilerParams(vmem_limit_bytes=(12 if rows <= 256 else 48) * MIB),
        cost_estimate=pl.CostEstimate(
            flops=0, bytes_accessed=0, transcendentals=0
        ),
        name="experts",
    )(
        *[array if array.shape[0] == 1 else in_vmem(array) for array in arrays[:-1]],
        in_hbm(down) if loads else in_vmem(down),
    )


def place_rows(source_refs, target_ref, segments, first, columns, table_ref=None):
    half, rows = columns.size, target_ref.shape[0]
    pieces = [(ref, *piece) for ref, group in zip(source_refs, segments) for piece in group]
    for source_ref, source, m, start, flip in pieces:
        at = pl.multiple_of(start + (lax.axis_index("tp") ^ flip) * m, m)
        own, others = pl.ds(at, m), pl.ds(rows // 2 + at, m)
        upper, lower = slice(source, source + m), slice(source + m, source + 2 * m)
        for to, at in ((own, upper), (others, lower)) if first else ((own, lower), (others, upper)):
            target_ref[to, columns] = source_ref[at, :half]
            if table_ref is not None:
                table_ref[to, :] = source_ref[at, half:].astype(f32)


def start_kernel(segments, *refs):
    *mine, gain_ref, gate_ref, up_ref, partial_ref, rows_ref = refs
    half, hidden = rows_ref.shape[1], gate_ref.shape[2]
    place_rows(mine, rows_ref, segments, True, pl.ds(0, half))
    at = pl.ds(pl.multiple_of(lax.axis_index("sp") * half, LANES), half)
    scaled = (rows_ref[...].astype(f32) * gain_ref[:, at]).astype(bf16)
    for e in range(gate_ref.shape[0]):
        for i, weight_ref in enumerate((gate_ref, up_ref)):
            to = slice((2 * e + i) * hidden, (2 * e + i + 1) * hidden)
            partial_ref[:, to] = jnp.dot(scaled, weight_ref[e, at, :], preferred_element_type=f32)


def finish_kernel(
    experts, first_of, segments, window, *refs
):
    count = len(segments)
    mine, other = refs[:count], refs[count : 2 * count]
    partial_ref, gain_ref, gate_ref, up_ref, down_ref, keep_ref, send_ref, *refs = refs[2 * count :]
    *stream_ref, rows_ref, table_ref = refs
    rows, width = rows_ref.shape
    half, hidden = width // 2, gate_ref.shape[2]
    sp_index = lax.axis_index("sp")
    my_cols = pl.ds(pl.multiple_of(sp_index * half, LANES), half)
    other_cols = pl.ds(pl.multiple_of((1 - sp_index) * half, LANES), half)
    place_rows(mine, rows_ref, segments, True, my_cols, table_ref)
    place_rows(other, rows_ref, segments, False, other_cols)
    for out_ref in stream_ref:
        count, cut = out_ref.shape
        at = pl.ds(pl.multiple_of(lax.axis_index("tp") * cut, LANES), cut)
        out_ref[...] = rows_ref[:count, at]
    values = rows_ref[...].astype(f32)
    inverse = lax.rsqrt(jnp.mean(values * values, axis=1, keepdims=True) + norm_epsilon)
    scaled = (rows_ref[:, other_cols].astype(f32) * gain_ref[:, other_cols]).astype(bf16)
    first_expert = first_of(lax.axis_index("ep"), sp_index)
    table = table_ref[...]
    lane = lax.broadcasted_iota(jnp.int32, table.shape, 1)
    total = None
    for e in range(gate_ref.shape[0]):
        wanted = (lane == first_expert + e) | (lane == first_expert + e + experts)
        scale = jnp.sum(jnp.where(wanted, table, 0.0), axis=1, keepdims=True)
        sums = []
        for i, weight_ref in enumerate((gate_ref, up_ref)):
            at = slice((2 * e + i) * hidden, (2 * e + i + 1) * hidden)
            begun = jnp.concatenate(
                [
                    partial_ref[start + window : start + window + rows // 2, at]
                    for start in (0, partial_ref.shape[0] // 2)
                ],
                axis=0,
            )
            rest = jnp.dot(scaled, weight_ref[e, other_cols, :], preferred_element_type=f32)
            sums.append((begun + rest) * inverse)
        gate, up = sums
        acts = (gate / (1.0 + jnp.exp(-gate)) * up * scale).astype(bf16)
        term = jnp.dot(acts, down_ref[e], preferred_element_type=f32)
        total = term if total is None else total + term
    keep_ref[...] = total[: rows // 2]
    send_ref[...] = total[rows // 2 :].astype(bf16)


def start_experts(mine, segments, gain, gate, up):
    rows = sum(array.shape[0] for array in mine)
    return pl.pallas_call(
        functools.partial(start_kernel, segments),
        in_specs=[WHOLE] * (len(mine) + 3),
        out_specs=WHOLE,
        out_shape=pltpu.VMEM((rows, 2 * gate.shape[0] * gate.shape[2]), f32),
        scratch_shapes=[pltpu.VMEM((rows, gain.shape[1] // 2), bf16)],
        compiler_params=pltpu.CompilerParams(vmem_limit_bytes=12 * MIB),
        cost_estimate=FREE,
        name="start_experts",
    )(*map(in_vmem, mine), gain, in_vmem(gate), in_vmem(up))


def finish_experts(
    mine, other, partial, segments, window, count, gain, gate, up, down, experts, n_sp, stream_shape
):
    width, local = gain.shape[1], gate.shape[0]
    segments = tuple(
        tuple(
            (source, m, start - window, flip)
            for source, m, start, flip in group
            if window <= start < window + count
        )
        for group in segments
    )
    return pl.pallas_call(
        functools.partial(
            finish_kernel, experts, lambda e, s: (e * n_sp + s) * local, segments, window
        ),
        in_specs=[WHOLE] * (2 * len(mine) + 5),
        out_specs=[WHOLE] * (3 if stream_shape else 2),
        out_shape=[
            pltpu.VMEM((count, width), f32),
            pltpu.VMEM((count, width), bf16),
            *([pltpu.VMEM(stream_shape, bf16)] if stream_shape else []),
        ],
        scratch_shapes=[
            pltpu.VMEM((2 * count, width), bf16),
            pltpu.VMEM((2 * count, mine[0].shape[1] - width // 2), f32),
        ],
        compiler_params=pltpu.CompilerParams(vmem_limit_bytes=12 * MIB),
        cost_estimate=FREE,
        name="finish_experts",
    )(*map(in_vmem, (*mine, *other, partial)), gain, *map(in_vmem, (gate, up, down)))


def split_kernel(keep, back, *out_refs):
    count = len(out_refs) // 2
    tp_index = lax.axis_index("tp")
    rows, width = out_refs[0].shape
    mine = pl.ds(pl.multiple_of(tp_index * width, LANES), width)
    theirs = pl.ds(pl.multiple_of((1 - tp_index) * width, LANES), width)
    for i, (keep_ref, send_ref) in enumerate(zip(out_refs[:count], out_refs[count:])):
        at = slice(i * rows, (i + 1) * rows)
        keep_ref[...] = keep[at, mine] + back[at, mine].astype(f32)
        send_ref[...] = (keep[at, theirs] + back[at, theirs].astype(f32)).astype(bf16)


def split(pieces, keep, back):
    shape = (keep.shape[0] // pieces, keep.shape[1] // 2)
    return pl.pallas_call(
        split_kernel,
        in_specs=[WHOLE] * 2,
        out_specs=[WHOLE] * (2 * pieces),
        out_shape=[pltpu.VMEM(shape, f32)] * pieces + [pltpu.VMEM(shape, bf16)] * pieces,
        compiler_params=pltpu.CompilerParams(vmem_limit_bytes=8 * MIB),
        cost_estimate=FREE,
        name="split",
    )(in_vmem(keep), in_vmem(back))


def part_kernel(keep, back, keep_ref, send_ref):
    rows = keep_ref.shape[0]
    keep_ref[...] = keep[:rows, :] + back[:rows, :].astype(f32)
    send_ref[...] = (keep[rows:, :] + back[rows:, :].astype(f32)).astype(bf16)


def part_near(keep, back):
    shape = (keep.shape[0] // 2, keep.shape[1])
    return pl.pallas_call(
        part_kernel,
        in_specs=[WHOLE] * 2,
        out_specs=[WHOLE] * 2,
        out_shape=[pltpu.VMEM(shape, f32), pltpu.VMEM(shape, bf16)],
        compiler_params=pltpu.CompilerParams(vmem_limit_bytes=8 * MIB),
        cost_estimate=FREE,
        name="part_near",
    )(in_vmem(keep), in_vmem(back))


def swap(array, axis, by=1):
    size = lax.axis_size(axis)
    return lax.ppermute(array, axis, [(i, i ^ by) for i in range(size)])


def shards(
    query,
    key_cache,
    value_cache,
    new_key,
    new_value,
    lengths,
    out_weight,
    residual,
    norm_gain,
    expert_ids,
    gate_weights,
    w_gate,
    w_up,
    w_down,
):
    rows = query.shape[0]
    width = residual.shape[1]
    n_ep, n_tp, n_sp = lax.axis_size("ep"), lax.axis_size("tp"), lax.axis_size("sp")
    tp_index = lax.axis_index("tp")
    experts = w_gate.shape[0] * n_ep * n_sp
    half = width // n_sp
    part = rows // n_tp
    out_width = width // n_tp
    heads_width = query.shape[1]

    packed, base, weight = attend(
        query, key_cache, value_cache, new_key, new_value, lengths, residual, expert_ids,
        gate_weights, out_weight, experts, n_sp
    )
    packed_other = swap(packed, "sp")
    stream_shape = (rows, out_width)
    if (n_ep, n_tp) == (4, 2) and part % 16 == 0:
        send_first, send_last, keep_first, keep_last, table_first, table_last = project(
            packed, packed_other, base, weight
        )
        first, last = swap(send_first, "tp"), swap(send_last, "tp")
        w_gate, _ = lax.optimization_barrier((w_gate, send_first))
        (w_gate,) = load(w_gate)
        first, w_gate = lax.optimization_barrier((first, w_gate))
        piece = jnp.concatenate([(keep_first + first.astype(f32)).astype(bf16), table_first], axis=1)
        second, third = swap(piece, "ep", 2), swap(piece, "ep", 3)
        piece_far = jnp.concatenate([(keep_last + last.astype(f32)).astype(bf16), table_last], axis=1)
        chip = jnp.concatenate([piece, piece_far], axis=0)
        next_chip = swap(chip, "ep", 1)
        w_up, _ = lax.optimization_barrier((w_up, chip))
        (w_up,) = load(w_up)
        second, w_up = lax.optimization_barrier((second, w_up))
        second_far, third_far = swap(second, "tp"), swap(third, "tp")
        w_down, _, _ = lax.optimization_barrier((w_down, second, third))
        (w_down,) = load(w_down)
        next_chip, w_down = lax.optimization_barrier((next_chip, w_down))
        second_far, third_far, w_down = lax.optimization_barrier((second_far, third_far, w_down))
        near = jnp.concatenate([chip, next_chip, second, third], axis=0)
        far = jnp.concatenate([second_far, third_far], axis=0)
        mine = (near, far)
        other = (swap(near, "sp"), swap(far, "sp"))
        size = 2 * part
        segments = tuple(
            tuple((i * size, part, k * rows, flip) for i, (k, flip) in enumerate(blocks))
            for blocks in (
                [(0, 0), (0, 1), (1, 0), (1, 1), (2, 0), (3, 0)],
                [(2, 1), (3, 1)],
            )
        )
        gain = norm_gain.reshape(1, width)
        partial = start_experts(mine, segments, gain, w_gate, w_up)
        keep, send = finish_experts(
            mine, other, partial, segments, 2 * rows, 2 * rows, gain, w_gate, w_up, w_down,
            experts, n_sp, None
        )
        partial, send = lax.optimization_barrier((partial, send))
        back = swap(send, "sp")
        keep_near, send_near, own_stream = finish_experts(
            mine, other, partial, segments, 0, 2 * rows, gain, w_gate, w_up, w_down,
            experts, n_sp, stream_shape
        )
        keep_second, keep_third, send_second, send_third = split(2, keep, back)
        second = keep_second + swap(send_second, "tp").astype(f32)
        third = keep_third + swap(send_third, "tp").astype(f32)
        second, third = swap(second.astype(bf16), "ep", 2), swap(third.astype(bf16), "ep", 3)
        keep_near, nearest = part_near(keep_near, swap(send_near, "sp"))
        keep_near, send_near = split(1, keep_near, swap(nearest, "ep", 1))
        final = own_stream.astype(f32) + second.astype(f32) + third.astype(f32)
        (final,) = lax.optimization_barrier((final,))
        return (final + keep_near + swap(send_near, "tp").astype(f32)).astype(bf16)

    def block_of(array, index):
        blocks = array.reshape(2, n_tp, part, -1)
        return lax.dynamic_slice_in_dim(blocks, index, 1, 1).reshape(2 * part, -1)

    def columns_of(array, index):
        return lax.dynamic_slice_in_dim(array, index * out_width, out_width, array.ndim - 1)

    both = jnp.concatenate([packed, packed_other], axis=0)
    terms = jnp.dot(both[:, :heads_width], weight, preferred_element_type=f32)
    residual_both = jnp.concatenate([base, packed_other[:, heads_width : heads_width + half]], axis=0)
    stream = block_of(terms, tp_index) + block_of(residual_both, tp_index).astype(f32)
    for by in range(1, n_tp):
        stream = stream + swap(block_of(terms, tp_index ^ by).astype(bf16), "tp", by).astype(f32)
    table = block_of(both[:, heads_width + half :], tp_index)
    piece = jnp.concatenate([stream.astype(bf16), table], axis=1)
    mine, places = [], []
    for by in range(n_ep):
        arrived = swap(piece, "ep", by) if by else piece
        for flip in range(n_tp):
            mine.append(swap(arrived, "tp", flip) if flip else arrived)
            places.append(((0, part, by * rows, flip),))
    if part % 16:
        gathered = jnp.stack(mine).reshape(n_ep, n_tp, 2, part, -1)
        bit = 1
        while bit < n_tp:
            flipped = gathered[:, jnp.array([j ^ bit for j in range(n_tp)])]
            gathered = jnp.where(tp_index & bit, flipped, gathered)
            bit *= 2
        mine = [gathered.transpose(2, 0, 1, 3, 4).reshape(2 * n_ep * rows, -1)]
        places = [((0, n_ep * rows, 0, None),)]
    other = [swap(array, "sp") for array in mine]
    keep, send, own_stream = run_experts(
        mine, other, tuple(places), norm_gain, w_gate, w_up, w_down, experts, n_sp, stream_shape, False
    )
    mixture = (keep + swap(send, "sp").astype(f32)).reshape(n_ep, rows, width)
    sums = columns_of(mixture, tp_index)
    for by in range(1, n_tp):
        sums = sums + swap(columns_of(mixture, tp_index ^ by).astype(bf16), "tp", by).astype(f32)
    final = sums[0]
    for by in range(1, n_ep):
        final = final + swap(sums[by].astype(bf16), "ep", by).astype(f32)
    return (final + own_stream.astype(f32)).astype(bf16)


def solution(mesh):
    placed = (
        P(("groups", "ep", "sp"), "tp"),
        P(("groups", "ep", "sp"), None, None),
        P(("groups", "ep", "sp"), None, None),
        P(("groups", "ep", "sp"), None),
        P(("groups", "ep", "sp"), None),
        P(("groups", "ep", "sp")),
        P("tp", "sp"),
        P(("groups", "ep", "sp"), None),
        P(),
        P(("groups", "ep", "sp"), None),
        P(("groups", "ep", "sp"), None),
        P(("ep", "sp"), None, "tp"),
        P(("ep", "sp"), None, "tp"),
        P(("ep", "sp"), "tp", None),
    )
    return jax.shard_map(
        shards,
        mesh=mesh,
        in_specs=placed,
        out_specs=P(("groups", "ep", "sp"), "tp"),
        check_vma=False,
    )
```

```python
import functools

import jax
import jax.numpy as jnp
from jax import lax
from jax.experimental import pallas as pl
from jax.experimental.pallas import tpu as pltpu
from jax.sharding import PartitionSpec as P

HEADS = 32
KV_HEADS = 4
HD = 128
LANES = 128
MIB = 2**20

masked_fill = -1e30
norm_epsilon = 1e-06
bf16 = jnp.bfloat16
f32 = jnp.float32


def attention_kernel(
    kv_count, per_group, chunk, experts, kv_block_of, lengths_hbm, query_hbm, key_hbm, value_hbm,
    new_key_hbm, new_value_hbm, residual_hbm, ids_hbm, gates_hbm, weight_hbm,
    packed_ref, base_ref, weight_ref,
    query_ref, key_ref, value_ref, new_key_ref, new_value_ref, residual_ref, ids_ref, gates_ref,
    rows_ref, lengths_ref, small_sems, cache_sems, weight_sem,
):
    rows, cached, kv_width = key_ref.shape
    heads = kv_count * per_group
    half = base_ref.shape[1]
    chunks = rows // chunk
    kv_at = pl.multiple_of(kv_block_of(lax.axis_index("tp")) * kv_width, HD)
    sp_index = lax.axis_index("sp")
    kv_cols = pl.ds(kv_at, kv_width)
    small = [
        pltpu.make_async_copy(source, target, small_sems.at[i])
        for i, (source, target) in enumerate(
            [
                (query_hbm, query_ref),
                (new_key_hbm.at[:, kv_cols], new_key_ref),
                (new_value_hbm.at[:, kv_cols], new_value_ref),
                (lengths_hbm, lengths_ref),
                (residual_hbm, residual_ref),
                (ids_hbm, ids_ref),
                (gates_hbm, gates_ref),
            ]
        )
    ]
    for copy in small[:4]:
        copy.start()
    cache_copies = []
    for i in range(chunks):
        at = pl.ds(i * chunk, chunk)
        pair = [
            pltpu.make_async_copy(
                source.at[at, :, kv_cols], target.at[at], cache_sems.at[which, i]
            )
            for which, (source, target) in enumerate(
                [(key_hbm, key_ref), (value_hbm, value_ref)]
            )
        ]
        for copy in pair:
            copy.start()
        cache_copies.append(pair)
    for copy in small[4:]:
        copy.start()
    weight_copy = pltpu.make_async_copy(weight_hbm, weight_ref, weight_sem)
    weight_copy.start()
    for copy in small[:4]:
        copy.wait()

    scaling = HD ** (-0.5)
    position = lax.broadcasted_iota(jnp.int32, (heads, cached), 1)
    for head in range(heads):
        kv, group = head // per_group, head % per_group
        rows_ref[kv, pl.ds(group, rows, stride=per_group), :] = query_ref[
            :, head * HD : (head + 1) * HD
        ].astype(f32)
    blank = jnp.zeros((per_group, HD), f32)
    for i in range(chunks):
        cache_copies[i][0].wait()
        scores, own = [], []
        for row in range(i * chunk, (i + 1) * chunk):
            at = slice(row * per_group, (row + 1) * per_group)
            queries = jnp.concatenate(
                [
                    jnp.concatenate(
                        [rows_ref[kv, at, :] if kv == other else blank for other in range(kv_count)],
                        axis=1,
                    )
                    for kv in range(kv_count)
                ],
                axis=0,
            )
            score = lax.dot_general(
                queries.astype(bf16),
                key_ref[row],
                (((1,), (1,)), ((), ())),
                preferred_element_type=f32,
            )
            visible = position < lengths_ref[row]
            scores.append(jnp.where(visible, score * scaling, masked_fill))
            fresh = new_key_ref[row : row + 1, :].astype(f32)
            own.append(jnp.sum(queries * fresh, axis=1, keepdims=True) * scaling)
        scores = jnp.concatenate(scores, axis=0)
        own = jnp.concatenate(own, axis=0)
        peak = jnp.maximum(jnp.max(scores, axis=1, keepdims=True), own)
        weights = jnp.exp(scores - peak)
        own_weight = jnp.exp(own - peak)
        inverse = 1.0 / (jnp.sum(weights, axis=1, keepdims=True) + own_weight)
        weights = weights.astype(bf16)
        cache_copies[i][1].wait()
        for row in range(i * chunk, (i + 1) * chunk):
            at = slice((row - i * chunk) * heads, (row - i * chunk + 1) * heads)
            blended = jnp.dot(weights[at], value_ref[row], preferred_element_type=f32)
            fresh = new_value_ref[row : row + 1, :].astype(f32)
            blended = (blended + own_weight[at] * fresh) * inverse[at]
            for kv in range(kv_count):
                rows_ref[kv, row * per_group : (row + 1) * per_group, :] = blended[
                    kv * per_group : (kv + 1) * per_group, kv * HD : (kv + 1) * HD
                ]
    for copy in small[4:]:
        copy.wait()
    width = heads * HD
    for head in range(heads):
        kv, group = head // per_group, head % per_group
        packed_ref[:, head * HD : (head + 1) * HD] = rows_ref[
            kv, pl.ds(group, rows, stride=per_group), :
        ].astype(bf16)
    packed_ref[:, width : width + half] = residual_ref[
        :, pl.ds(pl.multiple_of((1 - sp_index) * half, LANES), half)
    ]
    base_ref[...] = residual_ref[:, pl.ds(pl.multiple_of(sp_index * half, LANES), half)]
    spare = packed_ref.shape[1] - width - half
    place = lax.broadcasted_iota(jnp.int32, (spare, rows), 0)
    expert = jnp.where(place < experts, place, place - experts)
    table = jnp.zeros((spare, rows), f32)
    for k in range(ids_ref.shape[0]):
        table = table + jnp.where(ids_ref[k : k + 1, :] == expert, gates_ref[k : k + 1, :], 0.0)
    high = table.astype(bf16).astype(f32)
    table = jnp.where(place < experts, high, table - high)
    packed_ref[:, width + half :] = table.T.astype(bf16)
    weight_copy.wait()


def in_hbm(array):
    return pltpu.with_memory_space_constraint(array, pltpu.HBM)


def in_vmem(array):
    return pltpu.with_memory_space_constraint(array, pltpu.VMEM)


FREE = pl.CostEstimate(flops=0, bytes_accessed=0, transcendentals=0)
ANYWHERE = pl.BlockSpec(memory_space=pl.ANY)
WHOLE = pl.BlockSpec(memory_space=pltpu.VMEM)


def attend(
    query, key_cache, value_cache, new_key, new_value, lengths, residual, expert_ids,
    gate_weights, out_weight, experts, n_sp
):
    rows, width = query.shape
    cached = key_cache.shape[1]
    heads = width // HD
    grouping = HEADS // KV_HEADS
    kv_count = max(1, heads // grouping)
    per_group = heads // kv_count
    kv_width = kv_count * HD

    def kv_block_of(tp_index):
        return tp_index * heads // grouping // kv_count

    half = residual.shape[1] // n_sp
    spare = -(-2 * experts // LANES) * LANES
    chunk = min(16, rows)
    arrays = [
        lengths, query, key_cache, value_cache, new_key, new_value, residual, expert_ids.T,
        gate_weights.T, out_weight
    ]
    return pl.pallas_call(
        functools.partial(attention_kernel, kv_count, per_group, chunk, experts, kv_block_of),
        in_specs=[ANYWHERE] * len(arrays),
        out_specs=[WHOLE] * 3,
        out_shape=[
            pltpu.VMEM((rows, width + half + spare), bf16),
            pltpu.VMEM((rows, half), bf16),
            pltpu.VMEM(out_weight.shape, bf16),
        ],
        scratch_shapes=[
            pltpu.VMEM((rows, width), bf16),
            pltpu.VMEM((rows, cached, kv_width), bf16),
            pltpu.VMEM((rows, cached, kv_width), bf16),
            pltpu.VMEM((rows, kv_width), bf16),
            pltpu.VMEM((rows, kv_width), bf16),
            pltpu.VMEM(residual.shape, bf16),
            pltpu.VMEM((expert_ids.shape[1], rows), jnp.int32),
            pltpu.VMEM((expert_ids.shape[1], rows), f32),
            pltpu.VMEM((kv_count, rows * per_group, HD), f32),
            pltpu.SMEM((rows,), jnp.int32),
            pltpu.SemaphoreType.DMA((7,)),
            pltpu.SemaphoreType.DMA((2, rows // chunk)),
            pltpu.SemaphoreType.DMA,
        ],
        compiler_params=pltpu.CompilerParams(vmem_limit_bytes=24 * MIB),
        cost_estimate=FREE,
        name="attention",
    )(*map(in_hbm, arrays))


def project_kernel(
    packed_ref, other_ref, base_ref, weight_ref, send_first, send_last, keep_first, keep_last,
    table_first, table_last, terms_ref
):
    rows, half = base_ref.shape
    width = weight_ref.shape[0]
    part = rows // 2
    tp_index = lax.axis_index("tp")
    both = jnp.concatenate([packed_ref[:, :width], other_ref[:, :width]], axis=0)
    terms_ref[...] = jnp.dot(both, weight_ref[...], preferred_element_type=f32)
    for block, send_ref, keep_ref, table_ref in (
        (tp_index, send_last, keep_first, table_first),
        (1 - tp_index, send_first, keep_last, table_last),
    ):
        own = pl.ds(pl.multiple_of(block * part, part), part)
        for i, residual in enumerate((base_ref[own, :], other_ref[own, width : width + half])):
            to = slice(i * part, (i + 1) * part)
            terms = terms_ref[pl.ds(pl.multiple_of(i * rows + block * part, part), part), :]
            send_ref[to, :] = terms.astype(bf16)
            keep_ref[to, :] = terms + residual.astype(f32)
        table_ref[:part, :] = packed_ref[own, width + half :]
        table_ref[part:, :] = other_ref[own, width + half :]


def project(packed, packed_other, base, weight):
    shape = base.shape
    table = (shape[0], packed.shape[1] - weight.shape[0] - shape[1])
    return pl.pallas_call(
        project_kernel,
        in_specs=[WHOLE] * 4,
        out_specs=[WHOLE] * 6,
        out_shape=[
            *[pltpu.VMEM(shape, bf16)] * 2,
            *[pltpu.VMEM(shape, f32)] * 2,
            *[pltpu.VMEM(table, bf16)] * 2,
        ],
        scratch_shapes=[pltpu.VMEM((2 * shape[0], shape[1]), f32)],
        compiler_params=pltpu.CompilerParams(vmem_limit_bytes=8 * MIB),
        cost_estimate=FREE,
        name="project",
    )(*map(in_vmem, (packed, packed_other, base, weight)))


def load_kernel(*refs):
    *arrays, sems = refs
    count = len(arrays) // 2
    copies = [
        pltpu.make_async_copy(arrays[i], arrays[count + i], sems.at[i]) for i in range(count)
    ]
    for copy in copies:
        copy.start()
    for copy in copies:
        copy.wait()


def load(*arrays):
    return pl.pallas_call(
        load_kernel,
        in_specs=[ANYWHERE] * len(arrays),
        out_specs=[WHOLE] * len(arrays),
        out_shape=[pltpu.VMEM(array.shape, array.dtype) for array in arrays],
        scratch_shapes=[pltpu.SemaphoreType.DMA((len(arrays),))],
        compiler_params=pltpu.CompilerParams(vmem_limit_bytes=16 * MIB),
        cost_estimate=pl.CostEstimate(
            flops=0, bytes_accessed=0, transcendentals=0
        ),
        name="load_weights",
    )(*map(in_hbm, arrays))


def experts_kernel(experts, first_of, places, streams, loads, *refs):
    count = len(places)
    mine, other = refs[:count], refs[count : 2 * count]
    gain_ref, gate_ref, up_ref, down_ref, keep_ref, send_ref, *refs = refs[2 * count :]
    stream_ref = refs.pop(0) if streams else None
    if loads:
        down_hbm, down_ref, rows_ref, table_ref, sem = down_ref, *refs
        down_copy = pltpu.make_async_copy(down_hbm, down_ref, sem)
        down_copy.start()
    else:
        rows_ref, table_ref = refs
    half = rows_ref.shape[1] // 2
    rows = rows_ref.shape[0]
    sp_index = lax.axis_index("sp")
    tp_index = lax.axis_index("tp")
    my_cols = pl.ds(pl.multiple_of(sp_index * half, LANES), half)
    other_cols = pl.ds(pl.multiple_of((1 - sp_index) * half, LANES), half)
    for a, b, segments in zip(mine, other, places):
        for source, m, start, flip in segments:
            at = start if flip is None else pl.multiple_of(start + (tp_index ^ flip) * m, m)
            own, others = pl.ds(at, m), pl.ds(rows // 2 + at, m)
            upper, lower = slice(source, source + m), slice(source + m, source + 2 * m)
            rows_ref[own, my_cols] = a[upper, :half]
            rows_ref[others, my_cols] = a[lower, :half]
            rows_ref[own, other_cols] = b[lower, :half]
            rows_ref[others, other_cols] = b[upper, :half]
            table_ref[own, :] = a[upper, half:].astype(f32)
            table_ref[others, :] = a[lower, half:].astype(f32)
    if streams:
        count, width = stream_ref.shape
        out_cols = pl.ds(pl.multiple_of(tp_index * width, LANES), width)
        stream_ref[...] = rows_ref[:count, out_cols]
    values = rows_ref[...].astype(f32)
    inverse = lax.rsqrt(jnp.mean(values * values, axis=1, keepdims=True) + norm_epsilon)
    rows_ref[...] = (values * inverse * gain_ref[...]).astype(bf16)
    first_expert = first_of(lax.axis_index("ep"), sp_index)
    table = table_ref[...]
    lane = lax.broadcasted_iota(jnp.int32, table.shape, 1)
    hidden = []
    for e in range(gate_ref.shape[0]):
        wanted = (lane == first_expert + e) | (lane == first_expert + e + experts)
        scale = jnp.sum(jnp.where(wanted, table, 0.0), axis=1, keepdims=True)
        normed = rows_ref[...]
        gate = jnp.dot(normed, gate_ref[e], preferred_element_type=f32)
        up = jnp.dot(normed, up_ref[e], preferred_element_type=f32)
        hidden.append((gate / (1.0 + jnp.exp(-gate)) * up * scale).astype(bf16))
    if loads:
        down_copy.wait()
    total = None
    for e, acts in enumerate(hidden):
        term = jnp.dot(acts, down_ref[e], preferred_element_type=f32)
        total = term if total is None else total + term
    keep_ref[...] = total[: rows // 2]
    send_ref[...] = total[rows // 2 :].astype(bf16)


def run_experts(mine, other, places, gain, gate, up, down, experts, n_sp, stream_shape, loads):
    rows = sum(array.shape[0] for array in mine)
    width = gain.shape[0]
    local = gate.shape[0]
    arrays = [*mine, *other, gain.reshape(1, width), gate, up, down]
    extra = [pltpu.VMEM(stream_shape, bf16)] if stream_shape else []
    if loads:
        extra.append(pltpu.VMEM(down.shape, bf16))
    return pl.pallas_call(
        functools.partial(
            experts_kernel, experts, lambda e, s: (e * n_sp + s) * local, places, stream_shape is not None, loads
        ),
        in_specs=[WHOLE] * (len(arrays) - 1) + [ANYWHERE if loads else WHOLE],
        out_specs=[WHOLE] * (2 + len(extra)),
        out_shape=[
            pltpu.VMEM((rows // 2, width), f32),
            pltpu.VMEM((rows // 2, width), bf16),
            *extra,
        ],
        scratch_shapes=[
            pltpu.VMEM((rows, width), bf16),
            pltpu.VMEM((rows, mine[0].shape[1] - width // 2), f32),
        ]
        + ([pltpu.SemaphoreType.DMA] if loads else []),
        compiler_params=pltpu.CompilerParams(vmem_limit_bytes=(12 if rows <= 256 else 48) * MIB),
        cost_estimate=pl.CostEstimate(
            flops=0, bytes_accessed=0, transcendentals=0
        ),
        name="experts",
    )(
        *[array if array.shape[0] == 1 else in_vmem(array) for array in arrays[:-1]],
        in_hbm(down) if loads else in_vmem(down),
    )


def place_rows(source_refs, target_ref, segments, first, columns, table_ref=None):
    half, rows = columns.size, target_ref.shape[0]
    pieces = [(ref, *piece) for ref, group in zip(source_refs, segments) for piece in group]
    for source_ref, source, m, start, flip in pieces:
        at = pl.multiple_of(start + (lax.axis_index("tp") ^ flip) * m, m)
        own, others = pl.ds(at, m), pl.ds(rows // 2 + at, m)
        upper, lower = slice(source, source + m), slice(source + m, source + 2 * m)
        for to, at in ((own, upper), (others, lower)) if first else ((own, lower), (others, upper)):
            target_ref[to, columns] = source_ref[at, :half]
            if table_ref is not None:
                table_ref[to, :] = source_ref[at, half:].astype(f32)


def start_kernel(segments, *refs):
    *mine, gain_ref, gate_ref, up_ref, partial_ref, rows_ref = refs
    half, hidden = rows_ref.shape[1], gate_ref.shape[2]
    place_rows(mine, rows_ref, segments, True, pl.ds(0, half))
    at = pl.ds(pl.multiple_of(lax.axis_index("sp") * half, LANES), half)
    scaled = (rows_ref[...].astype(f32) * gain_ref[:, at]).astype(bf16)
    for e in range(gate_ref.shape[0]):
        for i, weight_ref in enumerate((gate_ref, up_ref)):
            to = slice((2 * e + i) * hidden, (2 * e + i + 1) * hidden)
            partial_ref[:, to] = jnp.dot(scaled, weight_ref[e, at, :], preferred_element_type=f32)


def finish_kernel(
    experts, first_of, segments, window, *refs
):
    count = len(segments)
    mine, other = refs[:count], refs[count : 2 * count]
    partial_ref, gain_ref, gate_ref, up_ref, down_ref, keep_ref, send_ref, *refs = refs[2 * count :]
    *stream_ref, rows_ref, table_ref = refs
    rows, width = rows_ref.shape
    half, hidden = width // 2, gate_ref.shape[2]
    sp_index = lax.axis_index("sp")
    my_cols = pl.ds(pl.multiple_of(sp_index * half, LANES), half)
    other_cols = pl.ds(pl.multiple_of((1 - sp_index) * half, LANES), half)
    place_rows(mine, rows_ref, segments, True, my_cols, table_ref)
    place_rows(other, rows_ref, segments, False, other_cols)
    for out_ref in stream_ref:
        count, cut = out_ref.shape
        at = pl.ds(pl.multiple_of(lax.axis_index("tp") * cut, LANES), cut)
        out_ref[...] = rows_ref[:count, at]
    values = rows_ref[...].astype(f32)
    inverse = lax.rsqrt(jnp.mean(values * values, axis=1, keepdims=True) + norm_epsilon)
    scaled = (rows_ref[:, other_cols].astype(f32) * gain_ref[:, other_cols]).astype(bf16)
    first_expert = first_of(lax.axis_index("ep"), sp_index)
    table = table_ref[...]
    lane = lax.broadcasted_iota(jnp.int32, table.shape, 1)
    total = None
    for e in range(gate_ref.shape[0]):
        wanted = (lane == first_expert + e) | (lane == first_expert + e + experts)
        scale = jnp.sum(jnp.where(wanted, table, 0.0), axis=1, keepdims=True)
        sums = []
        for i, weight_ref in enumerate((gate_ref, up_ref)):
            at = slice((2 * e + i) * hidden, (2 * e + i + 1) * hidden)
            begun = jnp.concatenate(
                [
                    partial_ref[start + window : start + window + rows // 2, at]
                    for start in (0, partial_ref.shape[0] // 2)
                ],
                axis=0,
            )
            rest = jnp.dot(scaled, weight_ref[e, other_cols, :], preferred_element_type=f32)
            sums.append((begun + rest) * inverse)
        gate, up = sums
        acts = (gate / (1.0 + jnp.exp(-gate)) * up * scale).astype(bf16)
        term = jnp.dot(acts, down_ref[e], preferred_element_type=f32)
        total = term if total is None else total + term
    keep_ref[...] = total[: rows // 2]
    send_ref[...] = total[rows // 2 :].astype(bf16)


def start_experts(mine, segments, gain, gate, up):
    rows = sum(array.shape[0] for array in mine)
    return pl.pallas_call(
        functools.partial(start_kernel, segments),
        in_specs=[WHOLE] * (len(mine) + 3),
        out_specs=WHOLE,
        out_shape=pltpu.VMEM((rows, 2 * gate.shape[0] * gate.shape[2]), f32),
        scratch_shapes=[pltpu.VMEM((rows, gain.shape[1] // 2), bf16)],
        compiler_params=pltpu.CompilerParams(vmem_limit_bytes=12 * MIB),
        cost_estimate=FREE,
        name="start_experts",
    )(*map(in_vmem, mine), gain, in_vmem(gate), in_vmem(up))


def finish_experts(
    mine, other, partial, segments, window, count, gain, gate, up, down, experts, n_sp, stream_shape
):
    width, local = gain.shape[1], gate.shape[0]
    segments = tuple(
        tuple(
            (source, m, start - window, flip)
            for source, m, start, flip in group
            if window <= start < window + count
        )
        for group in segments
    )
    return pl.pallas_call(
        functools.partial(
            finish_kernel, experts, lambda e, s: (e * n_sp + s) * local, segments, window
        ),
        in_specs=[WHOLE] * (2 * len(mine) + 5),
        out_specs=[WHOLE] * (3 if stream_shape else 2),
        out_shape=[
            pltpu.VMEM((count, width), f32),
            pltpu.VMEM((count, width), bf16),
            *([pltpu.VMEM(stream_shape, bf16)] if stream_shape else []),
        ],
        scratch_shapes=[
            pltpu.VMEM((2 * count, width), bf16),
            pltpu.VMEM((2 * count, mine[0].shape[1] - width // 2), f32),
        ],
        compiler_params=pltpu.CompilerParams(vmem_limit_bytes=12 * MIB),
        cost_estimate=FREE,
        name="finish_experts",
    )(*map(in_vmem, (*mine, *other, partial)), gain, *map(in_vmem, (gate, up, down)))


def split_kernel(keep, back, *out_refs):
    count = len(out_refs) // 2
    tp_index = lax.axis_index("tp")
    rows, width = out_refs[0].shape
    mine = pl.ds(pl.multiple_of(tp_index * width, LANES), width)
    theirs = pl.ds(pl.multiple_of((1 - tp_index) * width, LANES), width)
    for i, (keep_ref, send_ref) in enumerate(zip(out_refs[:count], out_refs[count:])):
        at = slice(i * rows, (i + 1) * rows)
        keep_ref[...] = keep[at, mine] + back[at, mine].astype(f32)
        send_ref[...] = (keep[at, theirs] + back[at, theirs].astype(f32)).astype(bf16)


def split(pieces, keep, back):
    shape = (keep.shape[0] // pieces, keep.shape[1] // 2)
    return pl.pallas_call(
        split_kernel,
        in_specs=[WHOLE] * 2,
        out_specs=[WHOLE] * (2 * pieces),
        out_shape=[pltpu.VMEM(shape, f32)] * pieces + [pltpu.VMEM(shape, bf16)] * pieces,
        compiler_params=pltpu.CompilerParams(vmem_limit_bytes=8 * MIB),
        cost_estimate=FREE,
        name="split",
    )(in_vmem(keep), in_vmem(back))


def part_kernel(keep, back, keep_ref, send_ref):
    rows = keep_ref.shape[0]
    keep_ref[...] = keep[:rows, :] + back[:rows, :].astype(f32)
    send_ref[...] = (keep[rows:, :] + back[rows:, :].astype(f32)).astype(bf16)


def part_near(keep, back):
    shape = (keep.shape[0] // 2, keep.shape[1])
    return pl.pallas_call(
        part_kernel,
        in_specs=[WHOLE] * 2,
        out_specs=[WHOLE] * 2,
        out_shape=[pltpu.VMEM(shape, f32), pltpu.VMEM(shape, bf16)],
        compiler_params=pltpu.CompilerParams(vmem_limit_bytes=8 * MIB),
        cost_estimate=FREE,
        name="part_near",
    )(in_vmem(keep), in_vmem(back))


def swap(array, axis, by=1):
    size = lax.axis_size(axis)
    return lax.ppermute(array, axis, [(i, i ^ by) for i in range(size)])


def shards(
    query,
    key_cache,
    value_cache,
    new_key,
    new_value,
    lengths,
    out_weight,
    residual,
    norm_gain,
    expert_ids,
    gate_weights,
    w_gate,
    w_up,
    w_down,
):
    rows = query.shape[0]
    width = residual.shape[1]
    n_ep, n_tp, n_sp = lax.axis_size("ep"), lax.axis_size("tp"), lax.axis_size("sp")
    tp_index = lax.axis_index("tp")
    experts = w_gate.shape[0] * n_ep * n_sp
    half = width // n_sp
    part = rows // n_tp
    out_width = width // n_tp
    heads_width = query.shape[1]

    packed, base, weight = attend(
        query, key_cache, value_cache, new_key, new_value, lengths, residual, expert_ids,
        gate_weights, out_weight, experts, n_sp
    )
    packed_other = swap(packed, "sp")
    stream_shape = (rows, out_width)
    if (n_ep, n_tp) == (4, 2) and part % 16 == 0:
        send_first, send_last, keep_first, keep_last, table_first, table_last = project(
            packed, packed_other, base, weight
        )
        first, last = swap(send_first, "tp"), swap(send_last, "tp")
        w_gate, _ = lax.optimization_barrier((w_gate, send_first))
        (w_gate,) = load(w_gate)
        first, w_gate = lax.optimization_barrier((first, w_gate))
        piece = jnp.concatenate([(keep_first + first.astype(f32)).astype(bf16), table_first], axis=1)
        second, third = swap(piece, "ep", 2), swap(piece, "ep", 3)
        piece_far = jnp.concatenate([(keep_last + last.astype(f32)).astype(bf16), table_last], axis=1)
        chip = jnp.concatenate([piece, piece_far], axis=0)
        next_chip = swap(chip, "ep", 1)
        w_up, _ = lax.optimization_barrier((w_up, chip))
        (w_up,) = load(w_up)
        third, w_up = lax.optimization_barrier((third, w_up))
        second_far, third_far = swap(second, "tp"), swap(third, "tp")
        w_down, _, _ = lax.optimization_barrier((w_down, second, third))
        (w_down,) = load(w_down)
        next_chip, w_down = lax.optimization_barrier((next_chip, w_down))
        second_far, third_far, w_down = lax.optimization_barrier((second_far, third_far, w_down))
        near = jnp.concatenate([chip, next_chip, second, third], axis=0)
        far = jnp.concatenate([second_far, third_far], axis=0)
        mine = (near, far)
        other = (swap(near, "sp"), swap(far, "sp"))
        size = 2 * part
        segments = tuple(
            tuple((i * size, part, k * rows, flip) for i, (k, flip) in enumerate(blocks))
            for blocks in (
                [(0, 0), (0, 1), (1, 0), (1, 1), (2, 0), (3, 0)],
                [(2, 1), (3, 1)],
            )
        )
        gain = norm_gain.reshape(1, width)
        partial = start_experts(mine, segments, gain, w_gate, w_up)
        keep, send = finish_experts(
            mine, other, partial, segments, 2 * rows, 2 * rows, gain, w_gate, w_up, w_down,
            experts, n_sp, None
        )
        partial, send = lax.optimization_barrier((partial, send))
        back = swap(send, "sp")
        keep_near, send_near, own_stream = finish_experts(
            mine, other, partial, segments, 0, 2 * rows, gain, w_gate, w_up, w_down,
            experts, n_sp, stream_shape
        )
        keep_second, keep_third, send_second, send_third = split(2, keep, back)
        second = keep_second + swap(send_second, "tp").astype(f32)
        third = keep_third + swap(send_third, "tp").astype(f32)
        second, third = swap(second.astype(bf16), "ep", 2), swap(third.astype(bf16), "ep", 3)
        keep_near, nearest = part_near(keep_near, swap(send_near, "sp"))
        keep_near, send_near = split(1, keep_near, swap(nearest, "ep", 1))
        final = own_stream.astype(f32) + second.astype(f32) + third.astype(f32)
        (final,) = lax.optimization_barrier((final,))
        return (final + keep_near + swap(send_near, "tp").astype(f32)).astype(bf16)

    def block_of(array, index):
        blocks = array.reshape(2, n_tp, part, -1)
        return lax.dynamic_slice_in_dim(blocks, index, 1, 1).reshape(2 * part, -1)

    def columns_of(array, index):
        return lax.dynamic_slice_in_dim(array, index * out_width, out_width, array.ndim - 1)

    both = jnp.concatenate([packed, packed_other], axis=0)
    terms = jnp.dot(both[:, :heads_width], weight, preferred_element_type=f32)
    residual_both = jnp.concatenate([base, packed_other[:, heads_width : heads_width + half]], axis=0)
    stream = block_of(terms, tp_index) + block_of(residual_both, tp_index).astype(f32)
    for by in range(1, n_tp):
        stream = stream + swap(block_of(terms, tp_index ^ by).astype(bf16), "tp", by).astype(f32)
    table = block_of(both[:, heads_width + half :], tp_index)
    piece = jnp.concatenate([stream.astype(bf16), table], axis=1)
    mine, places = [], []
    for by in range(n_ep):
        arrived = swap(piece, "ep", by) if by else piece
        for flip in range(n_tp):
            mine.append(swap(arrived, "tp", flip) if flip else arrived)
            places.append(((0, part, by * rows, flip),))
    if part % 16:
        gathered = jnp.stack(mine).reshape(n_ep, n_tp, 2, part, -1)
        bit = 1
        while bit < n_tp:
            flipped = gathered[:, jnp.array([j ^ bit for j in range(n_tp)])]
            gathered = jnp.where(tp_index & bit, flipped, gathered)
            bit *= 2
        mine = [gathered.transpose(2, 0, 1, 3, 4).reshape(2 * n_ep * rows, -1)]
        places = [((0, n_ep * rows, 0, None),)]
    other = [swap(array, "sp") for array in mine]
    keep, send, own_stream = run_experts(
        mine, other, tuple(places), norm_gain, w_gate, w_up, w_down, experts, n_sp, stream_shape, False
    )
    mixture = (keep + swap(send, "sp").astype(f32)).reshape(n_ep, rows, width)
    sums = columns_of(mixture, tp_index)
    for by in range(1, n_tp):
        sums = sums + swap(columns_of(mixture, tp_index ^ by).astype(bf16), "tp", by).astype(f32)
    final = sums[0]
    for by in range(1, n_ep):
        final = final + swap(sums[by].astype(bf16), "ep", by).astype(f32)
    return (final + own_stream.astype(f32)).astype(bf16)


def solution(mesh):
    placed = (
        P(("groups", "ep", "sp"), "tp"),
        P(("groups", "ep", "sp"), None, None),
        P(("groups", "ep", "sp"), None, None),
        P(("groups", "ep", "sp"), None),
        P(("groups", "ep", "sp"), None),
        P(("groups", "ep", "sp")),
        P("tp", "sp"),
        P(("groups", "ep", "sp"), None),
        P(),
        P(("groups", "ep", "sp"), None),
        P(("groups", "ep", "sp"), None),
        P(("ep", "sp"), None, "tp"),
        P(("ep", "sp"), None, "tp"),
        P(("ep", "sp"), "tp", None),
    )
    return jax.shard_map(
        shards,
        mesh=mesh,
        in_specs=placed,
        out_specs=P(("groups", "ep", "sp"), "tp"),
        check_vma=False,
    )
```
